256 devices in a mesh: group: 32 (over z, y), seq: 2 (over x_lo), tensor: 4 (over x_hi, core).
Axes of the slice: x: 4 (x_hi: 2, x_lo: 2; x = x_hi * 2 + x_lo), y: 4, z: 8, core: 2. Of those that a mesh axis runs over, the one named last changes fastest.
Arguments:
- stream: bfloat16 [3072, 5120], P(('group', 'seq')), may hold values from -2 to 2
- entering: bfloat16 [96, 5120], P('seq', 'tensor'), may hold values from -2 to 2
- qkv_weight: bfloat16 [5120, 3, 2560], P('seq', None, 'tensor'), as said below
- out_weight: bfloat16 [2560, 5120], P('tensor', 'seq'), may hold values from -0.25 to 0.25
- q_gain: float32 [2560], P('tensor'), may hold values from 1 to 5
- k_gain: float32 [2560], P('tensor'), may hold values from 1 to 5
- mod_table: float32 [48, 3, 5120], replicated, may hold values from -3 to 3
- levels: int32 [32], replicated, may hold values from 0 to 47
- frames: int32 [32], replicated, may hold values from 1 to 3, 64 in all
- block_mask: int32 [32, 32], replicated, may hold values 0 or 1
Outputs:
- moved: bfloat16 [3072, 5120], P(('group', 'seq'), 'tensor')
The draws below stay inside these ranges and needn't reach their ends.
Inputs may be any that keep to these rules, and one draw needn't show every extreme that they name: `qkv_weight`: entries of every projection have standard deviation about 5120 ** -0.5. `block_mask`: only entries below the diagonal are read.
All inputs are finite; a program needn't handle non-finite values.
Results may differ from the reference program's by a relative error of at most 0.015.
Values may be sent and summed in bfloat16 or wider, within the bound.
No kernel may reach another device: no remote copies, remote signals or barrier semaphores. Data moves between devices by JAX's collectives and lax.ppermute only.
A program may use at most 128 MiB of HBM per device.

```python
import math
import jax
import jax.numpy as jnp
import numpy as np
from jax import lax

D = 5120
HDIM = 128
H = 20
FRAMES = 3
FT = 32
LEVELS = 48
HD = 2560
BLOCK_TOK = 96
TOKENS = 3072
N_GROUP = 32


def draw_qkv_weight(key, part):
    key = jax.random.fold_in(key, 11)
    first, second, third = jax.random.split(key, 3)
    shared_part = jax.random.normal(first, (D, HD), jnp.float32)
    other_part = jax.random.normal(second, (D, HD), jnp.float32)
    value_part = jax.random.normal(third, (D, HD), jnp.float32)
    key_part = other_part
    stacked = jnp.stack([shared_part, key_part, value_part], axis=1)
    return (jnp.clip(stacked, -4.0, 4.0) * D ** (-0.5)).astype(jnp.bfloat16)


def draw_q_gain(key, part):
    key = jax.random.fold_in(key, 12)
    return jax.random.uniform(key, (HD,), jnp.float32, 1.0, 2.5)


def draw_k_gain(key, part):
    key = jax.random.fold_in(key, 13)
    return jax.random.uniform(key, (HD,), jnp.float32, 1.0, 2.5)


def touch_ends(result, own_key, least, high):
    spot = [jax.random.randint(jax.random.fold_in(own_key, axis), (), 0, length) for axis, length in enumerate(result.shape)]
    widest = result.shape.index(max(result.shape))
    beside = spot[:widest] + [(spot[widest] + 1) % result.shape[widest]] + spot[widest + 1:]
    return result.at[tuple(spot)].set(least).at[tuple(beside)].set(high)


def shard_levels(key, extent, cuts, least, high):
    gain, own = 1.0, jax.random.fold_in(key, 6)
    for position, shards_of in cuts:
        draws = jnp.exp(jax.random.uniform(jax.random.fold_in(own, position), (shards_of,), jnp.float32, least / len(cuts), high / len(cuts)))
        gain = gain * jnp.repeat(draws, extent[position] // shards_of).reshape([-1 if axis == position else 1 for axis in range(len(extent))])
    return gain


def profile(amount, total, bound, slope):
    weights = [(1 << 20) // math.isqrt(grade ** slope) + 1 for grade in range(2, amount + 1)]
    spare, holding = total - bound - (amount - 1), [1] * (amount - 1)
    while spare > 0:
        candidates = [i for i in range(amount - 1) if holding[i] < bound]
        pool, left = sum([weights[i] for i in candidates]), spare
        for i in candidates:
            extra = min(bound - holding[i], max(1, left * weights[i] // pool), spare)
            holding[i] = holding[i] + extra
            spare = spare - extra
    return np.array([bound] + holding)


def ragged_sizes(key, count, total, reach, slope):
    if count == 2:
        one = jax.random.randint(key, (), max(1, total - reach), min(reach, total - 1) + 1)
        return jnp.stack([one, total - one])
    sizes = jnp.asarray(profile(count, total, reach, slope), jnp.int32)
    couples = (count - 1) // 2
    source_of, sink = sizes[1:1 + 2 * couples:2], sizes[2:2 + 2 * couples:2]
    room = jnp.minimum(source_of - 1, reach - sink)
    moved = jax.random.randint(jax.random.fold_in(key, 1), (couples,), 0, 1 << 20) % (room + 1)
    sizes = sizes.at[1:1 + 2 * couples:2].set(source_of - moved).at[2:2 + 2 * couples:2].set(sink + moved)
    return sizes[jax.random.permutation(jax.random.fold_in(key, 2), count)]


def gaussian(key, dims, deviation, reach, cuts=(), kind=jnp.bfloat16):
    loudness = shard_levels(key, dims, cuts, -0.22, 0.18) if cuts else 1.0
    entries = jax.random.normal(key, dims, jnp.float32) * deviation * loudness
    return jnp.minimum(jnp.maximum(entries, -reach), reach).astype(kind)


def setup_inputs(seed: int = 0) -> dict:
    streams_of = jax.random.split(jax.random.key(seed), 11)
    return {
        "stream": gaussian(streams_of[0], (TOKENS, D), 0.3, 2.0, ((0, 64),)),
        "entering": gaussian(streams_of[1], (BLOCK_TOK, D), 0.3, 2.0, ((0, 2), (1, 4))),
        "qkv_weight": draw_qkv_weight(jax.random.fold_in(streams_of[10], 71), 0),
        "out_weight": gaussian(streams_of[3], (HD, D), (HD // 4) ** -0.5, 0.25, ((0, 4), (1, 2))),
        "q_gain": draw_q_gain(jax.random.fold_in(streams_of[10], 71), 0),
        "k_gain": draw_k_gain(jax.random.fold_in(streams_of[10], 71), 0),
        "mod_table": gaussian(streams_of[6], (LEVELS, 3, D), 0.6, 3.0, (), jnp.float32),
        "levels": touch_ends(jax.random.randint(streams_of[7], (N_GROUP,), 0, LEVELS), jax.random.fold_in(streams_of[7], 1), 0, LEVELS - 1).astype(jnp.int32),
        "frames": ragged_sizes(streams_of[8], N_GROUP, 2 * N_GROUP, FRAMES, 0).astype(jnp.int32),
        "block_mask": touch_ends((jax.random.randint(streams_of[9], (N_GROUP, N_GROUP), 0, 2) < 1).astype(jnp.int32), jax.random.fold_in(streams_of[9], 1), 0, 1),
    }


def layer_norm(values):
    center = lax.optimization_barrier(jnp.mean(values, axis=-1, keepdims=True))
    centred = values - center
    spread = lax.optimization_barrier(jnp.mean(centred * centred, axis=-1, keepdims=True))
    return centred * lax.rsqrt(spread + 1e-06)

def head_norm(values, gains):
    square = lax.optimization_barrier(jnp.mean(values * values, axis=-1, keepdims=True))
    return (values * lax.rsqrt(square + 1e-06) * gains).astype(jnp.bfloat16)

def reference(stream, entering, qkv_weight, out_weight, q_gain, k_gain, mod_table, levels, frames, block_mask):
    block_rows = FRAMES * FT
    level_hot = (levels[:, None] == jnp.arange(LEVELS, dtype=jnp.int32)[None, :]).astype(jnp.float32)
    modulation = jnp.einsum('cl,lkd->ckd', level_hot, mod_table, precision=lax.Precision.HIGHEST)
    values = stream.astype(jnp.float32).reshape(N_GROUP, block_rows, D)
    normed = (layer_norm(values) * (1.0 + modulation[:, 1:2, :]) + modulation[:, 0:1, :]).astype(jnp.bfloat16)
    normed = normed.reshape(TOKENS, D)
    projected = jnp.dot(normed, qkv_weight.reshape(D, 3 * HD), preferred_element_type=jnp.float32)
    projected = projected.reshape(TOKENS, 3, H, HDIM)
    queries = head_norm(projected[:, 0], q_gain.reshape(H, HDIM))
    key_rows = head_norm(projected[:, 1], k_gain.reshape(H, HDIM))
    value_rows = projected[:, 2].astype(jnp.bfloat16)
    positions = jnp.arange(TOKENS, dtype=jnp.int32)
    owner_order = jnp.arange(N_GROUP, dtype=jnp.int32)
    block_hot = (positions // block_rows)[:, None] == owner_order[None, :]
    key_frames = lax.optimization_barrier(jnp.sum(jnp.where(block_hot, frames[None, :], 0), axis=1))
    present = positions % block_rows < key_frames * FT
    allowed = (block_mask == 1) & (owner_order[None, :] < owner_order[:, None]) | (owner_order[None, :] == owner_order[:, None])
    key_wide = lax.optimization_barrier(key_rows).astype(jnp.float32)
    value_wide = lax.optimization_barrier(value_rows).astype(jnp.float32)
    score_scale = 1.0 / math.sqrt(HDIM)
    pieces = []
    for block_index in range(N_GROUP):
        query_wide = queries[block_index * block_rows:(block_index + 1) * block_rows].astype(jnp.float32)
        scores = jnp.einsum('qhd,khd->hqk', query_wide, key_wide) * score_scale
        live_mask = jnp.any(block_hot & allowed[block_index][None, :], axis=1) & present
        masked = jnp.where(live_mask[None, None, :], scores, -1e+30)
        row_max = lax.optimization_barrier(jnp.max(masked, axis=-1, keepdims=True))
        weights = jnp.where(live_mask[None, None, :], jnp.exp(masked - row_max), 0.0)
        weight_sum = lax.optimization_barrier(jnp.sum(weights, axis=-1))
        rounded = lax.optimization_barrier(weights.astype(jnp.bfloat16)).astype(jnp.float32)
        mixed = jnp.einsum('hqk,khd->qhd', rounded, value_wide)
        pieces.append((mixed / jnp.transpose(weight_sum)[:, :, None]).astype(jnp.bfloat16))
    attended = jnp.concatenate(pieces, axis=0).reshape(TOKENS, HD)
    projection = jnp.dot(attended, out_weight, preferred_element_type=jnp.float32).reshape(N_GROUP, block_rows, D)
    row_live = present.reshape(N_GROUP, block_rows, 1)
    updated = (values + jnp.where(row_live, modulation[:, 2:3, :] * projection, 0.0)).astype(jnp.bfloat16)
    updated = updated.reshape(TOKENS, D)
    return jnp.concatenate([entering, updated[:TOKENS - block_rows]], axis=0)
```

```python
import functools
import math

import jax
import jax.numpy as jnp
import numpy as np
from jax import lax
from jax.experimental import pallas as pl
from jax.experimental.pallas import tpu as pltpu
from jax.sharding import Mesh, PartitionSpec as P

HDIM = 128
FRAMES = 3
FT = 32
AXES = ("z", "y", "xl", "xh", "co")
SIZES = (8, 4, 2, 2, 2)
NZ, NY = 8, 4
HIDDEN = -(2.0**100)
STATS = 128


def moved(value, axes, target):
    sizes = [SIZES[AXES.index(axis)] for axis in axes]
    pairs = []
    for place in np.ndindex(*sizes):
        goal = target(*place)
        if goal is not None:
            pairs.append((int(np.ravel_multi_index(place, sizes)), int(np.ravel_multi_index(goal, sizes))))
    return lax.ppermute(value, axes, pairs)


def layer_norm(values):
    center = jnp.mean(values, axis=-1, keepdims=True)
    centred = values - center
    spread = jnp.mean(centred * centred, axis=-1, keepdims=True)
    return centred * lax.rsqrt(spread + 1e-06)


def head_norm(values, gains):
    square = jnp.mean(values * values, axis=-1, keepdims=True)
    return (values * lax.rsqrt(square + 1e-06) * gains).astype(jnp.bfloat16)


def attention_kernel(q_ref, own_ref, sib_ref, bias_ref, out_ref):
    blocks, rows, width = q_ref.shape
    heads = width // HDIM
    keys = own_ref.shape[0]
    bias = jnp.concatenate(
        [jnp.broadcast_to(bias_ref[b : b + 1, :], (rows, 2 * keys)) for b in range(blocks)], axis=0
    )
    stats = []
    for h in range(heads):
        at = pl.ds(h * HDIM, HDIM)
        past = pl.ds(width + h * HDIM, HDIM)
        q = q_ref[:, :, at].reshape(blocks * rows, HDIM)
        k = jnp.concatenate([own_ref[:, at], sib_ref[:, at]], axis=0)
        v = jnp.concatenate([own_ref[:, past], sib_ref[:, past]], axis=0)
        scores = lax.dot_general(q, k, (((1,), (1,)), ((), ())), preferred_element_type=jnp.float32)
        scores = scores * (1.0 / math.sqrt(HDIM)) + bias
        top = jnp.max(scores, axis=1, keepdims=True).astype(jnp.bfloat16).astype(jnp.float32)
        weights = jnp.exp(scores - top)
        total = jnp.sum(weights, axis=1, keepdims=True)
        mixed = jnp.dot(weights.astype(jnp.bfloat16), v, preferred_element_type=jnp.float32)
        out_ref[:, :, at] = mixed.astype(jnp.bfloat16).reshape(blocks, rows, HDIM)
        high = total.astype(jnp.bfloat16).astype(jnp.float32)
        stats += [top, high, total - high]
    lane = lax.broadcasted_iota(jnp.int32, (blocks * rows, STATS), 1)
    packed = jnp.zeros((blocks * rows, STATS), jnp.float32)
    for i, s in enumerate(stats):
        packed = jnp.where(lane == i, s, packed)
    out_ref[:, :, pl.ds(width, STATS)] = packed.astype(jnp.bfloat16).reshape(blocks, rows, STATS)


def merge_kernel(a_ref, b_ref, c_ref, d_ref, out_ref):
    rows, width = out_ref.shape
    parts = (a_ref, b_ref, c_ref, d_ref)
    stats = [p[:, pl.ds(width, STATS)].astype(jnp.float32) for p in parts]
    for h in range(width // HDIM):
        at = pl.ds(h * HDIM, HDIM)
        tops = [s[:, 3 * h : 3 * h + 1] for s in stats]
        sums = [s[:, 3 * h + 1 : 3 * h + 2] + s[:, 3 * h + 2 : 3 * h + 3] for s in stats]
        top = functools.reduce(jnp.maximum, tops)
        scales = [jnp.exp(t - top) for t in tops]
        total = sum(s * w for s, w in zip(sums, scales))
        mixed = sum(p[:, at].astype(jnp.float32) * w for p, w in zip(parts, scales))
        out_ref[:, at] = (mixed / total).astype(jnp.bfloat16)


def per_device(
    stream, entering, qkv_weight, out_weight, q_gain, k_gain, mod_table, levels, frames, block_mask
):
    z, y, xl, xh, co = (lax.axis_index(a) for a in AXES)
    group = z * NY + y
    rows, model = stream.shape
    width = q_gain.shape[0]
    heads = width // HDIM
    half = model // 2
    share = model // 4

    place = (2 * xh + co) * share
    before = moved(
        lax.dynamic_slice_in_dim(stream, place, share, 1),
        ("z", "y"),
        lambda a, b: None if (a, b) == (NZ - 1, NY - 1) else divmod(a * NY + b + 1, NY),
    )
    gains = jnp.stack([q_gain, k_gain])
    gains = jnp.where(co == xl, gains, moved(gains, ("co",), lambda c: (1 - c,)))

    shift = lax.dynamic_index_in_dim(mod_table, levels[group], 0, keepdims=False)
    normed = (layer_norm(stream.astype(jnp.float32)) * (1.0 + shift[1]) + shift[0]).astype(jnp.bfloat16)
    mine = lax.dynamic_slice_in_dim(normed, xl * half, half, 1)
    theirs = lax.dynamic_slice_in_dim(normed, (1 - xl) * half, half, 1)
    got = moved(theirs, ("xl",), lambda s: (1 - s,))
    project = lambda a: jnp.einsum(
        "rd,dkn->rkn", a, qkv_weight, preferred_element_type=jnp.float32
    ).astype(jnp.bfloat16)
    first = moved(project(mine), ("xl", "co"), lambda s, c: (c, s))
    second = moved(project(got), ("xl", "co"), lambda s, c: (c, 1 - s))
    projected = first.astype(jnp.float32) + second.astype(jnp.float32)

    shaped = projected.reshape(rows, 3, heads, HDIM)
    queries = head_norm(shaped[:, 0], gains[0].reshape(heads, HDIM)).reshape(rows, width)
    key_rows = head_norm(shaped[:, 1], gains[1].reshape(heads, HDIM)).reshape(rows, width)
    pair = jnp.concatenate([key_rows, shaped[:, 2].astype(jnp.bfloat16).reshape(rows, width)], axis=1)

    held = [pair]
    for d in range(1, NZ):
        held.append(moved(pair, ("z",), lambda a, d=d: (a + d,) if a + d < NZ else None))
    asked = [queries]
    for d in range(1, NY):
        asked.append(moved(queries, ("y",), lambda b, d=d: ((b + d) % NY,)))
    held = jnp.concatenate(held, axis=0)
    asked = jnp.stack(asked)
    beside = moved(held, ("co",), lambda c: (1 - c,))

    asker = z * NY + (y - jnp.arange(NY, dtype=jnp.int32)) % NY
    planes = z - jnp.arange(NZ, dtype=jnp.int32)
    key_block = planes * NY + y
    key_clip = jnp.maximum(key_block, 0)
    seen = block_mask[asker[:, None], key_clip[None, :]] == 1
    seen = (seen & (key_block[None, :] < asker[:, None])) | (key_block[None, :] == asker[:, None])
    seen = seen & (planes >= 0)[None, :]
    token = jnp.stack([co, 1 - co])[:, None] * rows + jnp.arange(rows, dtype=jnp.int32)[None, :]
    there = token[:, None, :] < FT * frames[key_clip][None, :, None]
    bias = jnp.where(seen[:, None, :, None] & there[None], 0.0, HIDDEN).astype(jnp.float32)
    bias = bias.reshape(NY, 2 * NZ * rows)

    partial = pl.pallas_call(
        attention_kernel,
        out_shape=jax.ShapeDtypeStruct((NY, rows, width + STATS), jnp.bfloat16),
        compiler_params=pltpu.CompilerParams(vmem_limit_bytes=32 * 1024 * 1024),
    )(asked, held, beside, bias)

    parts = []
    for d in range(NY):
        def target(a, b, d=d):
            goal = a * NY + (b - d) % NY + 1
            return None if goal == NZ * NY else divmod(goal, NY)

        parts.append(moved(partial[d], ("z", "y"), target))
    attended = pl.pallas_call(
        merge_kernel, out_shape=jax.ShapeDtypeStruct((rows, width), jnp.bfloat16)
    )(*parts)

    same = moved(attended, ("xl", "co"), lambda s, c: (c, s))
    other = moved(attended, ("xl", "co"), lambda s, c: (1 - c, s))
    both = jnp.concatenate([same, other], axis=0)
    out = jnp.dot(both, out_weight, preferred_element_type=jnp.float32)
    keep = lax.dynamic_slice_in_dim(out, co * share, share, 1)
    give = lax.dynamic_slice_in_dim(out, (1 - co) * share, share, 1).astype(jnp.bfloat16)
    keep = (keep + moved(give, ("co",), lambda c: (1 - c,)).astype(jnp.float32)).astype(jnp.bfloat16)
    keep = keep.reshape(2, rows, share)
    pieces = [
        moved(
            lax.dynamic_index_in_dim(keep, k ^ xh ^ xl, 0, keepdims=False),
            ("xl", "xh"),
            lambda s, h, k=k: (k ^ h, s),
        )
        for k in (0, 1)
    ]
    summed = pieces[0].astype(jnp.float32) + pieces[1].astype(jnp.float32)
    prior = jnp.maximum(group - 1, 0)
    gate = lax.dynamic_slice(mod_table, (levels[prior], 2, place), (1, 1, share)).reshape(1, share)
    live = xl * rows + jnp.arange(rows, dtype=jnp.int32) < frames[prior] * FT
    updated = before.astype(jnp.float32) + jnp.where(live[:, None], gate * summed, 0.0)
    return jnp.where(group == 0, entering, updated.astype(jnp.bfloat16))


def solution(mesh):
    fine = Mesh(mesh.devices.reshape(SIZES), AXES)
    tensor = ("xh", "co")
    placed = (
        P(("z", "y", "xl"), None),
        P("xl", tensor),
        P("xl", None, tensor),
        P(tensor, "xl"),
        P(tensor),
        P(tensor),
        P(),
        P(),
        P(),
        P(),
    )
    return jax.shard_map(
        per_device,
        mesh=fine,
        in_specs=placed,
        out_specs=P(("z", "y", "xl"), tensor),
        check_vma=False,
    )
```

```python
import functools
import math

import jax
import jax.numpy as jnp
import numpy as np
from jax import lax
from jax.experimental import pallas as pl
from jax.experimental.pallas import tpu as pltpu
from jax.sharding import Mesh, PartitionSpec as P

HDIM = 128
FT = 32
AXES = ("z", "y", "xl", "xh", "co")
SIZES = (8, 4, 2, 2, 2)
NZ, NY = 8, 4
HIDDEN = -(2.0**100)
STATS = 128
SMEM = pl.BlockSpec(memory_space=pltpu.SMEM)
VMEM = pl.BlockSpec(memory_space=pltpu.VMEM)
ANY = pl.BlockSpec(memory_space=pl.ANY)
HBM = pl.BlockSpec(memory_space=pltpu.HBM)


def room(mib):
    return pltpu.CompilerParams(vmem_limit_bytes=mib * 1024 * 1024)


def my_group():
    return lax.axis_index("z") * NY + lax.axis_index("y")


def like(shape, dtype=jnp.bfloat16):
    return jax.ShapeDtypeStruct(shape, dtype)


def moved(value, axes, target):
    sizes = [SIZES[AXES.index(axis)] for axis in axes]
    pairs = []
    for place in np.ndindex(*sizes):
        goal = target(*place)
        if goal is not None:
            pairs.append((int(np.ravel_multi_index(place, sizes)), int(np.ravel_multi_index(goal, sizes))))
    return lax.ppermute(value, axes, pairs)


def next_owner(z, y):
    goal = z * NY + y + 1
    return None if goal == NZ * NY else divmod(goal, NY)


def norm_kernel(levels, stream_ref, table_ref, mine_ref, theirs_ref, share_ref, raw, held, sems):
    rows, model = raw.shape
    half = model // 2
    share = share_ref.shape[1]
    whole = pltpu.make_async_copy(stream_ref, raw, sems.at[0])
    whole.start()
    level = levels[my_group()]
    begin = pl.multiple_of((level // 8) * 8, 8)
    copy = pltpu.make_async_copy(table_ref.at[pl.ds(0, 2), pl.ds(begin, 8), :], held, sems.at[1])
    copy.start()
    whole.wait()
    values = raw[...].astype(jnp.float32)
    center = jnp.mean(values, axis=-1, keepdims=True)
    centred = values - center
    spread = jnp.mean(centred * centred, axis=-1, keepdims=True)
    centred = centred * lax.rsqrt(spread + 1e-06)
    copy.wait()
    row = pl.ds(lax.rem(level, 8), 1)
    normed = (centred * (1.0 + held[1, row, :]) + held[0, row, :]).astype(jnp.bfloat16)

    @pl.when(lax.axis_index("xl") == 0)
    def _():
        mine_ref[...] = normed[:, :half]
        theirs_ref[...] = normed[:, half:]

    @pl.when(lax.axis_index("xl") == 1)
    def _():
        mine_ref[...] = normed[:, half:]
        theirs_ref[...] = normed[:, :half]

    place = (2 * lax.axis_index("xh") + lax.axis_index("co")) * share
    share_ref[...] = raw[:, pl.ds(pl.multiple_of(place, 128), share)]


def set_up(levels, frames, block_mask, table_ref, bias_ref, gate_ref, held, sem):
    blocks, keys = bias_ref.shape
    rows, share = gate_ref.shape
    z, y, core = lax.axis_index("z"), lax.axis_index("y"), lax.axis_index("co")
    columns = pl.ds(pl.multiple_of((2 * lax.axis_index("xh") + core) * share, 128), share)
    prior = jnp.maximum(my_group() - 1, 0)
    level = levels[prior]
    aligned = pl.multiple_of((level // 8) * 8, 8)
    copy = pltpu.make_async_copy(table_ref.at[2, pl.ds(aligned, 8), columns], held, sem)
    copy.start()
    lane = lax.broadcasted_iota(jnp.int32, (1, keys), 1)
    for b in range(blocks):
        asker = z * NY + lax.rem(y + NY - b, NY)
        line = jnp.full((1, keys), HIDDEN, jnp.float32)
        for half in range(2):
            first = rows * (core if half == 0 else 1 - core)
            for d in range(NZ):
                block = lax.rem(z + NZ - d, NZ) * NY + y
                seen = (block == asker) | ((block < asker) & (block_mask[asker, block] == 1))
                count = jnp.where(seen, jnp.clip(frames[block] * FT - first, 0, rows), 0)
                begin = (half * NZ + d) * rows
                line = jnp.where((lane >= begin) & (lane < begin + count), 0.0, line)
        bias_ref[pl.ds(b, 1), :] = line
    copy.wait()
    position = lax.axis_index("xl") * rows + lax.broadcasted_iota(jnp.int32, (rows, share), 0)
    gate = held[pl.ds(lax.rem(level, 8), 1), :]
    gate_ref[...] = jnp.where(position < frames[prior] * FT, gate, 0.0)


def project_kernel(first, tokens_ref, weight_ref, *rest):
    *outs, held, sems = rest
    slots, depth, width = held.shape
    steps = tokens_ref.shape[1] // depth
    copies = []
    for n in range(slots):
        j, i = divmod(n, steps)
        piece = weight_ref.at[first + j, pl.ds(i * depth, depth), :]
        copies.append(pltpu.make_async_copy(piece, held.at[n], sems.at[n]))
    for copy in copies:
        copy.start()
    done = 0
    for out in outs:
        for j in range(out.shape[1] // width):
            total = None
            for i in range(steps):
                copies[done].wait()
                term = jnp.dot(
                    tokens_ref[:, i * depth : (i + 1) * depth], held[done], preferred_element_type=jnp.float32
                )
                total = term if total is None else total + term
                done += 1
            out[:, pl.ds(j * width, width)] = total


def head_norm(values, gain):
    square = jnp.mean(values * values, axis=-1, keepdims=True)
    return (values * lax.rsqrt(square + 1e-06) * gain).astype(jnp.bfloat16)


def own_gain(which, at, own_ref, sib_ref):
    pick = lax.axis_index("co") == lax.axis_index("xl")
    return jnp.where(pick, own_ref[which : which + 1, at], sib_ref[which : which + 1, at])


def kv_kernel(a_ref, b_ref, own_ref, sib_ref, waits_ref, also_ref, out_ref):
    width = own_ref.shape[1]
    for h in range(width // HDIM):
        at = pl.ds(h * HDIM, HDIM)
        out_ref[:, at] = head_norm(a_ref[:, at] + b_ref[:, at], own_gain(1, at, own_ref, sib_ref))
    at = pl.ds(width, width)
    out_ref[:, at] = (a_ref[:, at] + b_ref[:, at]).astype(jnp.bfloat16)


def query_kernel(
    levels, frames, block_mask, a_ref, b_ref, own_ref, sib_ref, table_ref, waits_ref, out_ref, *rest
):
    for h in range(out_ref.shape[1] // HDIM):
        at = pl.ds(h * HDIM, HDIM)
        out_ref[:, at] = head_norm(a_ref[:, at] + b_ref[:, at], own_gain(0, at, own_ref, sib_ref))
    set_up(levels, frames, block_mask, table_ref, *rest)


def attention_kernel(*refs):
    asked, keys_in, bias_ref, outs = refs[:NY], refs[NY : NY + 2 * NZ], refs[NY + 2 * NZ], refs[-NY:]
    rows, width = asked[0].shape
    keys = NZ * rows
    blocks = len(asked)
    bias = jnp.concatenate(
        [jnp.broadcast_to(bias_ref[b : b + 1, :], (rows, 2 * keys)) for b in range(blocks)], axis=0
    )
    stats = []
    for h in range(width // HDIM):
        at = pl.ds(h * HDIM, HDIM)
        past = pl.ds(width + h * HDIM, HDIM)
        q = jnp.concatenate([r[:, at] for r in asked], axis=0)
        k = jnp.concatenate([r[:, at] for r in keys_in], axis=0)
        v = jnp.concatenate([r[:, past] for r in keys_in], axis=0)
        scores = lax.dot_general(q, k, (((1,), (1,)), ((), ())), preferred_element_type=jnp.float32)
        scores = scores * (1.0 / math.sqrt(HDIM)) + bias
        top = jnp.max(scores, axis=1, keepdims=True).astype(jnp.bfloat16).astype(jnp.float32)
        weights = jnp.exp(scores - top)
        total = jnp.sum(weights, axis=1, keepdims=True)
        mixed = jnp.dot(weights.astype(jnp.bfloat16), v, preferred_element_type=jnp.float32)
        mixed = mixed.astype(jnp.bfloat16)
        for b, out in enumerate(outs):
            out[:, at] = mixed[b * rows : (b + 1) * rows]
        high = total.astype(jnp.bfloat16).astype(jnp.float32)
        stats += [top, high, total - high]
    lane = lax.broadcasted_iota(jnp.int32, (blocks * rows, STATS), 1)
    packed = jnp.zeros((blocks * rows, STATS), jnp.float32)
    for i, s in enumerate(stats):
        packed = jnp.where(lane == i, s, packed)
    packed = packed.astype(jnp.bfloat16)
    for b, out in enumerate(outs):
        out[:, pl.ds(width, STATS)] = packed[b * rows : (b + 1) * rows]


def merge_kernel(a_ref, b_ref, c_ref, d_ref, out_ref):
    width = out_ref.shape[1]
    parts = (a_ref, b_ref, c_ref, d_ref)
    stats = [p[:, pl.ds(width, STATS)].astype(jnp.float32) for p in parts]
    for h in range(width // HDIM):
        at = pl.ds(h * HDIM, HDIM)
        tops = [s[:, 3 * h : 3 * h + 1] for s in stats]
        sums = [s[:, 3 * h + 1 : 3 * h + 2] + s[:, 3 * h + 2 : 3 * h + 3] for s in stats]
        top = functools.reduce(jnp.maximum, tops)
        scales = [jnp.exp(t - top) for t in tops]
        total = sum(s * w for s, w in zip(sums, scales))
        mixed = sum(p[:, at].astype(jnp.float32) * w for p, w in zip(parts, scales))
        out_ref[:, at] = (mixed / total).astype(jnp.bfloat16)


def out_kernel(same_ref, other_ref, weight_ref, keep_ref, give_ref):
    rows, share = same_ref.shape[0], keep_ref.shape[1]
    swap = lax.axis_index("xl") != lax.axis_index("xh")
    same, other = same_ref[...], other_ref[...]
    tokens = jnp.concatenate([jnp.where(swap, other, same), jnp.where(swap, same, other)], axis=0)
    core = lax.axis_index("co")
    near = weight_ref[:, pl.ds(pl.multiple_of(core * share, 128), share)]
    give = weight_ref[:, pl.ds(pl.multiple_of((1 - core) * share, 128), share)]
    give_ref[...] = jnp.dot(tokens, give, preferred_element_type=jnp.float32).astype(jnp.bfloat16)
    keep_ref[...] = jnp.dot(tokens, near, preferred_element_type=jnp.float32)


def per_device(
    stream, entering, qkv_weight, out_weight, q_gain, k_gain, mod_table, levels, frames, block_mask
):
    rows, model = stream.shape
    width = q_gain.shape[0]
    half, share = model // 2, model // 4
    keys = 2 * NZ * rows
    table = pltpu.with_memory_space_constraint(jnp.transpose(mod_table, (1, 0, 2)), pltpu.HBM)
    weight = pltpu.with_memory_space_constraint(jnp.transpose(qkv_weight, (1, 0, 2)), pltpu.HBM)

    mine, theirs, part = pl.pallas_call(
        norm_kernel,
        in_specs=[SMEM, HBM, HBM],
        out_specs=[VMEM] * 3,
        out_shape=[like((rows, half)), like((rows, half)), like((rows, share))],
        scratch_shapes=[
            pltpu.VMEM((rows, model), jnp.bfloat16),
            pltpu.VMEM((2, 8, model), jnp.float32),
            pltpu.SemaphoreType.DMA((2,)),
        ],
        compiler_params=room(8),
        name="norm",
    )(levels, pltpu.with_memory_space_constraint(stream, pltpu.HBM), table)
    before = moved(part, ("z", "y"), next_owner)
    got = moved(theirs, ("xl",), lambda s: (1 - s,))
    gains = jnp.stack([q_gain, k_gain])
    beside_gains = moved(gains, ("co",), lambda c: (1 - c,))

    def project(tokens, first, counts, name):
        steps = 4
        return pl.pallas_call(
            functools.partial(project_kernel, first),
            in_specs=[VMEM, HBM],
            out_specs=[VMEM] * len(counts),
            out_shape=[like((rows, count * width), jnp.float32) for count in counts],
            scratch_shapes=[
                pltpu.VMEM((sum(counts) * steps, half // steps, width), jnp.bfloat16),
                pltpu.SemaphoreType.DMA((sum(counts) * steps,)),
            ],
            compiler_params=room(4 + 4 * sum(counts)),
            name=name,
        )(tokens, weight)

    q_mine, kv_mine = project(mine, 0, (1, 2), "project_mine")
    kv_mine = moved(kv_mine, ("xl", "co"), lambda s, c: (c, s))
    q_mine = moved(q_mine, ("xl", "co"), lambda s, c: (c, s))
    (kv_got,) = project(got, 1, (2,), "project_kv")
    kv_got = moved(kv_got, ("xl", "co"), lambda s, c: (c, 1 - s))
    (q_got,) = project(got, 0, (1,), "project_q")
    pair = pl.pallas_call(
        kv_kernel,
        in_specs=[VMEM, VMEM, VMEM, VMEM, ANY, ANY],
        out_specs=VMEM,
        out_shape=like((rows, 2 * width)),
        compiler_params=room(4),
        name="kv_heads",
    )(kv_mine, kv_got, gains, beside_gains, q_got, before)
    q_got = moved(q_got, ("xl", "co"), lambda s, c: (c, 1 - s))

    held = [pair]
    for d in range(1, NZ):
        held.append(moved(pair, ("z",), lambda a, d=d: ((a + d) % NZ,)))
    beside = [moved(h, ("co",), lambda c: (1 - c,)) for h in held]

    queries, bias, gate = pl.pallas_call(
        query_kernel,
        in_specs=[SMEM, SMEM, SMEM, VMEM, VMEM, VMEM, VMEM, HBM, ANY],
        out_specs=[VMEM] * 3,
        out_shape=[
            like((rows, width)),
            like((NY, keys), jnp.float32),
            like((rows, share), jnp.float32),
        ],
        scratch_shapes=[pltpu.VMEM((8, share), jnp.float32), pltpu.SemaphoreType.DMA],
        compiler_params=room(6),
        name="q_heads",
    )(levels, frames, block_mask, q_mine, q_got, gains, beside_gains, table, beside[0])
    asked = [queries]
    for d in range(1, NY):
        asked.append(moved(queries, ("y",), lambda b, d=d: ((b + d) % NY,)))

    partial = pl.pallas_call(
        attention_kernel,
        in_specs=[VMEM] * (NY + 2 * NZ + 1),
        out_specs=[VMEM] * NY,
        out_shape=[like((rows, width + STATS))] * NY,
        compiler_params=room(16),
        name="attention",
    )(*asked, *held, *beside, bias)
    parts = [partial[0]]
    for d in range(1, NY):
        parts.append(moved(partial[d], ("y",), lambda b, d=d: ((b - d) % NY,)))
    attended = pl.pallas_call(
        merge_kernel, out_shape=like((rows, width)), compiler_params=room(4), name="merge"
    )(*parts)

    same = moved(attended, ("xl", "co"), lambda s, c: (c, s))
    other = moved(attended, ("xl", "co"), lambda s, c: (1 - c, s))
    keep, give = pl.pallas_call(
        out_kernel,
        in_specs=[VMEM, VMEM, VMEM],
        out_specs=[VMEM, VMEM],
        out_shape=[like((2 * rows, share), jnp.float32), like((2 * rows, share))],
        compiler_params=room(10),
        name="out",
    )(same, other, out_weight)
    keep = (keep + moved(give, ("co",), lambda c: (1 - c,)).astype(jnp.float32)).astype(jnp.bfloat16)

    def onward(k):
        def target(a, b, s, h):
            goal = next_owner(a, b)
            return None if goal is None else goal + (k ^ h, s)

        return target

    summed = sum(
        moved(keep[k * rows : (k + 1) * rows], ("z", "y", "xl", "xh"), onward(k)).astype(jnp.float32) for k in (0, 1)
    )
    updated = (before.astype(jnp.float32) + gate * summed).astype(jnp.bfloat16)
    return jnp.where(my_group() == 0, entering, updated)


def solution(mesh):
    fine = Mesh(mesh.devices.reshape(SIZES), AXES)
    tensor = ("xh", "co")
    placed = (
        P(("z", "y", "xl"), None),
        P("xl", tensor),
        P("xl", None, tensor),
        P(tensor, "xl"),
        P(tensor),
        P(tensor),
        P(),
        P(),
        P(),
        P(),
    )
    return jax.shard_map(
        per_device,
        mesh=fine,
        in_specs=placed,
        out_specs=P(("z", "y", "xl"), tensor),
        check_vma=False,
    )
```

```python
import functools
import math

import jax
import jax.numpy as jnp
import numpy as np
from jax import lax
from jax.experimental import pallas as pl
from jax.experimental.pallas import tpu as pltpu
from jax.sharding import Mesh, PartitionSpec as P

HDIM = 128
FT = 32
AXES = ("z", "y", "xl", "xh", "co")
SIZES = (8, 4, 2, 2, 2)
NZ, NY = 8, 4
HIDDEN = -(2.0**100)
STATS = 128
GAIN_ROWS = 8
ORDER = (0, 1, 7, 2, 6, 3, 5, 4)
SMEM = pl.BlockSpec(memory_space=pltpu.SMEM)
VMEM = pl.BlockSpec(memory_space=pltpu.VMEM)
ANY = pl.BlockSpec(memory_space=pl.ANY)
HBM = pl.BlockSpec(memory_space=pltpu.HBM)


def room(mib):
    return pltpu.CompilerParams(vmem_limit_bytes=mib * 1024 * 1024)


def my_group():
    return lax.axis_index("z") * NY + lax.axis_index("y")


def like(shape, dtype=jnp.bfloat16):
    return jax.ShapeDtypeStruct(shape, dtype)


def moved(value, axes, target):
    sizes = [SIZES[AXES.index(axis)] for axis in axes]
    pairs = []
    for place in np.ndindex(*sizes):
        goal = target(*place)
        if goal is not None:
            pairs.append((int(np.ravel_multi_index(place, sizes)), int(np.ravel_multi_index(goal, sizes))))
    return lax.ppermute(value, axes, pairs)


def next_owner(z, y):
    goal = z * NY + y + 1
    return None if goal == NZ * NY else divmod(goal, NY)


def after(value, *others):
    return pl.pallas_call(
        lambda *refs: None,
        in_specs=[ANY] * (1 + len(others)),
        out_specs=ANY,
        out_shape=like(value.shape, value.dtype),
        input_output_aliases={0: 0},
        compiler_params=room(1),
        name="after",
    )(value, *others)


def norm_kernel(levels, stream_ref, table_ref, mine_ref, theirs_ref, change_ref, share_ref, raw, held, sems):
    rows, model = raw.shape
    half, share = mine_ref.shape[1], share_ref.shape[1]
    whole = pltpu.make_async_copy(stream_ref, raw, sems.at[0])
    whole.start()
    level = levels[my_group()]
    begin = pl.multiple_of((level // 8) * 8, 8)
    seq = lax.axis_index("xl")
    columns = pl.ds(pl.multiple_of(seq * half, 128), half)
    copy = pltpu.make_async_copy(table_ref.at[pl.ds(0, 2), pl.ds(begin, 8), columns], held, sems.at[1])
    copy.start()
    whole.wait()
    values = raw[...].astype(jnp.float32)
    center = jnp.mean(values, axis=-1, keepdims=True)
    centred = values - center
    spread = jnp.mean(centred * centred, axis=-1, keepdims=True)
    scale = lax.rsqrt(spread + 1e-06)
    lane = lax.broadcasted_iota(jnp.int32, (rows, STATS), 1)
    terms = jnp.zeros((rows, STATS), jnp.float32)
    for i, left in enumerate((center, scale)):
        for j in range(3):
            term = left.astype(jnp.bfloat16).astype(jnp.float32)
            terms = jnp.where(lane == 3 * i + j, term, terms)
            left = left - term
    theirs_ref[:, pl.ds(0, half)] = raw[:, pl.ds(pl.multiple_of((1 - seq) * half, 128), half)]
    theirs_ref[:, pl.ds(half, STATS)] = terms.astype(jnp.bfloat16)
    copy.wait()
    row = pl.ds(lax.rem(level, 8), 1)
    change_ref[pl.ds(0, 1), :] = held[0, row, :]
    change_ref[pl.ds(1, 1), :] = 1.0 + held[1, row, :]
    own = raw[:, columns].astype(jnp.float32)
    mine_ref[...] = ((own - center) * scale * change_ref[1:2, :] + change_ref[0:1, :]).astype(jnp.bfloat16)
    place = (2 * seq + lax.axis_index("co")) * share
    share_ref[...] = raw[:, pl.ds(pl.multiple_of(place, 128), share)]


def set_up(levels, frames, block_mask, table_ref, bias_ref, gate_ref, held, sem):
    blocks, keys = bias_ref.shape
    rows, share = gate_ref.shape[0] // 2, gate_ref.shape[1]
    z, y, core = lax.axis_index("z"), lax.axis_index("y"), lax.axis_index("co")
    columns = pl.ds(pl.multiple_of((2 * lax.axis_index("xl") + core) * share, 128), share)
    level = levels[my_group()]
    aligned = pl.multiple_of((level // 8) * 8, 8)
    copy = pltpu.make_async_copy(table_ref.at[2, pl.ds(aligned, 8), columns], held, sem)
    copy.start()
    lane = lax.broadcasted_iota(jnp.int32, (1, keys), 1)
    for b in range(blocks):
        asker = z * NY + lax.rem(y + NY - b, NY)
        line = jnp.full((1, keys), HIDDEN, jnp.float32)
        for half in range(2):
            first = rows * (core if half == 0 else 1 - core)
            for i, d in enumerate(ORDER):
                block = lax.rem(z + NZ - d, NZ) * NY + y
                seen = (block == asker) | ((block < asker) & (block_mask[asker, block] == 1))
                count = jnp.where(seen, jnp.clip(frames[block] * FT - first, 0, rows), 0)
                begin = (half * NZ + i) * rows
                line = jnp.where((lane >= begin) & (lane < begin + count), 0.0, line)
        bias_ref[pl.ds(b, 1), :] = line
    copy.wait()
    gate = held[pl.ds(lax.rem(level, 8), 1), :]
    row = lax.broadcasted_iota(jnp.int32, (rows, share), 0)
    for k in range(2):
        position = (lax.axis_index("xh") if k == 0 else 1 - lax.axis_index("xh")) * rows + row
        gate_ref[pl.ds(k * rows, rows), :] = jnp.where(position < frames[my_group()] * FT, gate, 0.0)


def fetch(first, weight_ref, held, sems):
    slots, depth, _ = held.shape
    steps = weight_ref.shape[1] // depth
    copies = []
    for n in range(slots):
        j, i = divmod(n, steps)
        piece = weight_ref.at[first + j, pl.ds(i * depth, depth), :]
        copies.append(pltpu.make_async_copy(piece, held.at[n], sems.at[n]))
    for copy in copies:
        copy.start()
    return copies


def project(tokens_ref, copies, held, outs):
    rows, depth, width = tokens_ref.shape[0], held.shape[1], held.shape[2]
    steps = tokens_ref.shape[1] // depth
    done = 0
    for out in outs:
        for j in range(out.shape[1] // width):
            total = None
            for i in range(steps):
                copies[done].wait()
                part = tokens_ref[:, i * depth : (i + 1) * depth]
                term = jnp.dot(part, held[done], preferred_element_type=jnp.float32)
                total = term if total is None else total + term
                done += 1
            out[pl.ds(0, rows), pl.ds(j * width, width)] = total


def project_mine_kernel(tokens_ref, q_gain_ref, k_gain_ref, weight_ref, q_ref, kv_ref, held, sems):
    copies = fetch(0, weight_ref, held, sems)
    rows, width = tokens_ref.shape[0], q_ref.shape[1]
    for j, gain_ref in enumerate((k_gain_ref, q_gain_ref)):
        gain = jnp.broadcast_to(gain_ref[...].reshape(1, width), (GAIN_ROWS, width))
        kv_ref[pl.ds(rows, GAIN_ROWS), pl.ds(j * width, width)] = gain
    project(tokens_ref, copies, held, (q_ref, kv_ref))


def project_kv_kernel(got_ref, change_ref, share_ref, weight_ref, kv_ref, tokens_ref, rest_ref, held, sems):
    copies = fetch(1, weight_ref, held, sems)
    share, half = share_ref.shape[1], tokens_ref.shape[1]
    terms = got_ref[:, pl.ds(half, STATS)].astype(jnp.float32)
    center = terms[:, 0:1] + terms[:, 1:2] + terms[:, 2:3]
    scale = terms[:, 3:4] + terms[:, 4:5] + terms[:, 5:6]
    centred = got_ref[:, pl.ds(0, half)].astype(jnp.float32) - center
    tokens_ref[...] = (centred * scale * change_ref[1:2, :] + change_ref[0:1, :]).astype(jnp.bfloat16)
    other = got_ref[:, pl.ds(pl.multiple_of(lax.axis_index("co") * share, 128), share)]
    rest_ref[...] = jnp.where(lax.axis_index("xh") == lax.axis_index("xl"), share_ref[...], other)
    project(tokens_ref, copies, held, (kv_ref,))


def project_q_kernel(tokens_ref, weight_ref, q_ref, held, sems):
    project(tokens_ref, fetch(0, weight_ref, held, sems), held, (q_ref,))


def head_norm(values, gain):
    square = jnp.mean(values * values, axis=-1, keepdims=True)
    return (values * lax.rsqrt(square + 1e-06) * gain).astype(jnp.bfloat16)


def kv_kernel(a_ref, b_ref, waits_ref, out_ref):
    rows, width = out_ref.shape[0], out_ref.shape[1] // 2
    for h in range(width // HDIM):
        at = pl.ds(h * HDIM, HDIM)
        out_ref[:, at] = head_norm(a_ref[:rows, at] + b_ref[:, at], a_ref[rows : rows + 1, at])
    at = pl.ds(width, width)
    out_ref[:, at] = (a_ref[:rows, at] + b_ref[:, at]).astype(jnp.bfloat16)


def query_kernel(levels, frames, block_mask, a_ref, b_ref, kv_ref, table_ref, waits_ref, out_ref, *rest):
    rows, width = out_ref.shape
    for h in range(width // HDIM):
        at = pl.ds(h * HDIM, HDIM)
        gain = kv_ref[rows : rows + 1, pl.ds(width + h * HDIM, HDIM)]
        out_ref[:, at] = head_norm(a_ref[:, at] + b_ref[:, at], gain)
    set_up(levels, frames, block_mask, table_ref, *rest)


def attention_kernel(*refs):
    asked_ref, keys_in, bias_ref, outs = refs[0], refs[1 : 1 + 2 * NZ], refs[1 + 2 * NZ], refs[-NY:]
    rows, width = asked_ref.shape[1:]
    y = lax.axis_index("y")
    asked = [asked_ref.at[lax.rem(y + NY - b, NY)] for b in range(NY)]
    keys = NZ * rows
    blocks = len(asked)
    bias = jnp.concatenate(
        [jnp.broadcast_to(bias_ref[b : b + 1, :], (rows, 2 * keys)) for b in range(blocks)], axis=0
    )
    stats = []
    for h in range(width // HDIM):
        at = pl.ds(h * HDIM, HDIM)
        past = pl.ds(width + h * HDIM, HDIM)
        q = jnp.concatenate([r[:, at] for r in asked], axis=0)
        k = jnp.concatenate([r[:, at] for r in keys_in], axis=0)
        v = jnp.concatenate([r[:, past] for r in keys_in], axis=0)
        scores = lax.dot_general(q, k, (((1,), (1,)), ((), ())), preferred_element_type=jnp.float32)
        scores = scores * (1.0 / math.sqrt(HDIM)) + bias
        top = jnp.max(scores, axis=1, keepdims=True).astype(jnp.bfloat16).astype(jnp.float32)
        weights = jnp.exp(scores - top)
        total = jnp.sum(weights, axis=1, keepdims=True)
        mixed = jnp.dot(weights.astype(jnp.bfloat16), v, preferred_element_type=jnp.float32)
        mixed = mixed.astype(jnp.bfloat16)
        for b, out in enumerate(outs):
            out[:, at] = mixed[b * rows : (b + 1) * rows]
        high = total.astype(jnp.bfloat16).astype(jnp.float32)
        stats += [top, high, total - high]
    lane = lax.broadcasted_iota(jnp.int32, (blocks * rows, STATS), 1)
    packed = jnp.zeros((blocks * rows, STATS), jnp.float32)
    for i, s in enumerate(stats):
        packed = jnp.where(lane == i, s, packed)
    packed = packed.astype(jnp.bfloat16)
    for b, out in enumerate(outs):
        out[:, pl.ds(width, STATS)] = packed[b * rows : (b + 1) * rows]


def merge_kernel(a_ref, b_ref, c_ref, d_ref, out_ref):
    width = out_ref.shape[1]
    parts = (a_ref, b_ref, c_ref, d_ref)
    stats = [p[:, pl.ds(width, STATS)].astype(jnp.float32) for p in parts]
    for h in range(width // HDIM):
        at = pl.ds(h * HDIM, HDIM)
        tops = [s[:, 3 * h : 3 * h + 1] for s in stats]
        sums = [s[:, 3 * h + 1 : 3 * h + 2] + s[:, 3 * h + 2 : 3 * h + 3] for s in stats]
        top = functools.reduce(jnp.maximum, tops)
        scales = [jnp.exp(t - top) for t in tops]
        total = sum(s * w for s, w in zip(sums, scales))
        mixed = sum(p[:, at].astype(jnp.float32) * w for p, w in zip(parts, scales))
        out_ref[:, at] = (mixed / total).astype(jnp.bfloat16)


def out_kernel(same_ref, other_ref, weight_ref, keep_ref, give_ref):
    rows, share = same_ref.shape[0], keep_ref.shape[1]
    swap = lax.axis_index("xl") != lax.axis_index("xh")
    same, other = same_ref[...], other_ref[...]
    tokens = jnp.concatenate([jnp.where(swap, other, same), jnp.where(swap, same, other)], axis=0)
    core = lax.axis_index("co")
    near = weight_ref[:, pl.ds(pl.multiple_of(core * share, 128), share)]
    give = weight_ref[:, pl.ds(pl.multiple_of((1 - core) * share, 128), share)]
    give_ref[...] = jnp.dot(tokens, give, preferred_element_type=jnp.float32).astype(jnp.bfloat16)
    keep_ref[...] = jnp.dot(tokens, near, preferred_element_type=jnp.float32)


def pieces_kernel(keep_ref, got_ref, gate_ref, rest_ref, first_ref, second_ref):
    rows = first_ref.shape[0]
    change = gate_ref[...] * (keep_ref[...] + got_ref[...].astype(jnp.float32))
    first_ref[...] = (rest_ref[...].astype(jnp.float32) + change[:rows]).astype(jnp.bfloat16)
    second_ref[...] = change[rows:].astype(jnp.bfloat16)


def per_device(
    stream, entering, qkv_weight, out_weight, q_gain, k_gain, mod_table, levels, frames, block_mask
):
    rows, model = stream.shape
    width = q_gain.shape[0]
    half, share = model // 2, model // 4
    keys = 2 * NZ * rows
    table = pltpu.with_memory_space_constraint(jnp.transpose(mod_table, (1, 0, 2)), pltpu.HBM)
    weight = pltpu.with_memory_space_constraint(jnp.transpose(qkv_weight, (1, 0, 2)), pltpu.HBM)

    mine, theirs, change, part = pl.pallas_call(
        norm_kernel,
        in_specs=[SMEM, HBM, HBM],
        out_specs=[VMEM] * 4,
        out_shape=[
            like((rows, half)),
            like((rows, half + STATS)),
            like((2, half), jnp.float32),
            like((rows, share)),
        ],
        scratch_shapes=[
            pltpu.VMEM((rows, model), jnp.bfloat16),
            pltpu.VMEM((2, 8, half), jnp.float32),
            pltpu.SemaphoreType.DMA((2,)),
        ],
        compiler_params=room(8),
        name="norm",
    )(levels, pltpu.with_memory_space_constraint(stream, pltpu.HBM), table)
    theirs = moved(theirs, ("xl",), lambda s: (1 - s,))

    def weights(count):
        steps = 4
        return [
            pltpu.VMEM((count * steps, half // steps, width), jnp.bfloat16),
            pltpu.SemaphoreType.DMA((count * steps,)),
        ]

    q_mine, kv_mine = pl.pallas_call(
        project_mine_kernel,
        in_specs=[VMEM, VMEM, VMEM, HBM],
        out_specs=[VMEM] * 2,
        out_shape=[like((rows, width), jnp.float32), like((rows + GAIN_ROWS, 2 * width), jnp.float32)],
        scratch_shapes=weights(3),
        compiler_params=room(16),
        name="project_mine",
    )(mine, q_gain, k_gain, weight)
    kv_mine = moved(kv_mine, ("xl", "co"), lambda s, c: (c, s))
    q_mine = moved(q_mine, ("xl", "co"), lambda s, c: (c, s))
    kv_got, got, rest = pl.pallas_call(
        project_kv_kernel,
        in_specs=[VMEM, VMEM, VMEM, HBM],
        out_specs=[VMEM] * 3,
        out_shape=[like((rows, 2 * width), jnp.float32), like((rows, half)), like((rows, share))],
        scratch_shapes=weights(2),
        compiler_params=room(14),
        name="project_kv",
    )(theirs, change, part, weight)
    kv_got = moved(kv_got, ("xl", "co"), lambda s, c: (c, 1 - s))
    q_got = pl.pallas_call(
        project_q_kernel,
        in_specs=[VMEM, HBM],
        out_specs=VMEM,
        out_shape=like((rows, width), jnp.float32),
        scratch_shapes=weights(1),
        compiler_params=room(10),
        name="project_q",
    )(got, weight)
    pair = pl.pallas_call(
        kv_kernel,
        in_specs=[VMEM, VMEM, ANY],
        out_specs=VMEM,
        out_shape=like((rows, 2 * width)),
        compiler_params=room(4),
        name="kv_heads",
    )(kv_mine, kv_got, q_got)
    q_got = moved(q_got, ("xl", "co"), lambda s, c: (c, 1 - s))

    held = [pair]
    for d in ORDER[1:]:
        held.append(moved(pair, ("z",), lambda a, d=d: ((a + d) % NZ,)))

    queries, bias, gate = pl.pallas_call(
        query_kernel,
        in_specs=[SMEM, SMEM, SMEM, VMEM, VMEM, VMEM, HBM, ANY],
        out_specs=[VMEM] * 3,
        out_shape=[
            like((rows, width)),
            like((NY, keys), jnp.float32),
            like((2 * rows, share), jnp.float32),
        ],
        scratch_shapes=[pltpu.VMEM((8, share), jnp.float32), pltpu.SemaphoreType.DMA],
        compiler_params=room(6),
        name="q_heads",
    )(levels, frames, block_mask, q_mine, q_got, kv_mine, table, pair)
    asked = lax.all_gather(queries, "y")
    held = held[:1] + [after(h, asked) for h in held[1:]]
    beside = [moved(h, ("co",), lambda c: (1 - c,)) for h in held]

    partial = pl.pallas_call(
        attention_kernel,
        in_specs=[VMEM] * (2 * NZ + 2),
        out_specs=[VMEM] * NY,
        out_shape=[like((rows, width + STATS))] * NY,
        compiler_params=room(16),
        name="attention",
    )(asked, *held, *beside, bias)
    parts = [partial[0]]
    for d in range(1, NY):
        parts.append(moved(partial[d], ("y",), lambda b, d=d: ((b - d) % NY,)))
    attended = pl.pallas_call(
        merge_kernel, out_shape=like((rows, width)), compiler_params=room(4), name="merge"
    )(*parts)

    same = moved(attended, ("xl", "co"), lambda s, c: (c, s))
    other = moved(attended, ("xl", "co"), lambda s, c: (1 - c, s))
    keep, give = pl.pallas_call(
        out_kernel,
        in_specs=[VMEM, VMEM, VMEM],
        out_specs=[VMEM, VMEM],
        out_shape=[like((2 * rows, share), jnp.float32), like((2 * rows, share))],
        compiler_params=room(10),
        name="out",
    )(same, other, out_weight)
    first, second = pl.pallas_call(
        pieces_kernel,
        in_specs=[VMEM] * 4,
        out_specs=[VMEM] * 2,
        out_shape=[like((rows, share))] * 2,
        compiler_params=room(6),
        name="pieces",
    )(keep, moved(give, ("co",), lambda c: (1 - c,)), gate, rest)

    def onward(k):
        def target(a, b, s, h):
            goal = next_owner(a, b)
            return None if goal is None else goal + (k ^ h, s)

        return target

    first = moved(first, ("z", "y", "xl", "xh"), onward(0))
    second = moved(second, ("z", "y", "xl", "xh"), onward(1))
    updated = (first.astype(jnp.float32) + second.astype(jnp.float32)).astype(jnp.bfloat16)
    return jnp.where(my_group() == 0, entering, updated)


def solution(mesh):
    fine = Mesh(mesh.devices.reshape(SIZES), AXES)
    tensor = ("xh", "co")
    placed = (
        P(("z", "y", "xl"), None),
        P("xl", tensor),
        P("xl", None, tensor),
        P(tensor, "xl"),
        P(tensor),
        P(tensor),
        P(),
        P(),
        P(),
        P(),
    )
    return jax.shard_map(
        per_device,
        mesh=fine,
        in_specs=placed,
        out_specs=P(("z", "y", "xl"), tensor),
        check_vma=False,
    )
```

```python
import functools
import math

import jax
import jax.numpy as jnp
import numpy as np
from jax import lax
from jax.experimental import pallas as pl
from jax.experimental.pallas import tpu as pltpu
from jax.sharding import Mesh, PartitionSpec as P

HDIM = 128
FT = 32
AXES = ("z", "y", "xl", "xh", "co")
SIZES = (8, 4, 2, 2, 2)
NZ, NY = 8, 4
HIDDEN = -(2.0**100)
STATS = 128
GAIN_ROWS = 16
FAR = ((1, 7, 3, 5), (2, 6, 4))
SMEM = pl.BlockSpec(memory_space=pltpu.SMEM)
VMEM = pl.BlockSpec(memory_space=pltpu.VMEM)
ANY = pl.BlockSpec(memory_space=pl.ANY)
HBM = pl.BlockSpec(memory_space=pltpu.HBM)


def room(mib):
    return pltpu.CompilerParams(vmem_limit_bytes=mib * 1024 * 1024)


def my_group():
    return lax.axis_index("z") * NY + lax.axis_index("y")


def like(shape, dtype=jnp.bfloat16):
    return jax.ShapeDtypeStruct(shape, dtype)


def moved(value, axes, target):
    sizes = [SIZES[AXES.index(axis)] for axis in axes]
    pairs = []
    for place in np.ndindex(*sizes):
        goal = target(*place)
        if goal is not None:
            pairs.append((int(np.ravel_multi_index(place, sizes)), int(np.ravel_multi_index(goal, sizes))))
    return lax.ppermute(value, axes, pairs)


def next_owner(z, y):
    goal = z * NY + y + 1
    return None if goal == NZ * NY else divmod(goal, NY)


def after(value, *others):
    return pl.pallas_call(
        lambda *refs: None,
        in_specs=[ANY] * (1 + len(others)),
        out_specs=ANY,
        out_shape=like(value.shape, value.dtype),
        input_output_aliases={0: 0},
        compiler_params=room(1),
        name="after",
    )(value, *others)


def norm_kernel(levels_ref, stream_ref, table_ref, mine_ref, theirs_ref, change_ref, share_ref, levels, raw, held, sems):
    rows, model = raw.shape
    half, share = mine_ref.shape[1], share_ref.shape[1]
    whole = pltpu.make_async_copy(stream_ref, raw, sems.at[0])
    whole.start()
    first = pltpu.make_async_copy(levels_ref, levels, sems.at[2])
    first.start()
    first.wait()
    level = levels[my_group()]
    begin = pl.multiple_of((level // 8) * 8, 8)
    seq = lax.axis_index("xl")
    columns = pl.ds(pl.multiple_of(seq * half, 128), half)
    copy = pltpu.make_async_copy(table_ref.at[pl.ds(0, 2), pl.ds(begin, 8), columns], held, sems.at[1])
    copy.start()
    whole.wait()
    values = raw[...].astype(jnp.float32)
    center = jnp.mean(values, axis=-1, keepdims=True)
    centred = values - center
    spread = jnp.mean(centred * centred, axis=-1, keepdims=True)
    scale = lax.rsqrt(spread + 1e-06)
    lane = lax.broadcasted_iota(jnp.int32, (rows, STATS), 1)
    terms = jnp.zeros((rows, STATS), jnp.float32)
    for i, left in enumerate((center, scale)):
        for j in range(3):
            term = left.astype(jnp.bfloat16).astype(jnp.float32)
            terms = jnp.where(lane == 3 * i + j, term, terms)
            left = left - term
    quarter = (1 - seq) * half + lax.axis_index("co") * share
    theirs_ref[:, pl.ds(0, share)] = raw[:, pl.ds(pl.multiple_of(quarter, 128), share)]
    theirs_ref[:, pl.ds(share, STATS)] = terms.astype(jnp.bfloat16)
    copy.wait()
    row = pl.ds(lax.rem(level, 8), 1)
    change_ref[pl.ds(0, 1), :] = held[0, row, :]
    change_ref[pl.ds(1, 1), :] = 1.0 + held[1, row, :]
    own = raw[:, columns].astype(jnp.float32)
    mine_ref[...] = ((own - center) * scale * change_ref[1:2, :] + change_ref[0:1, :]).astype(jnp.bfloat16)
    place = (2 * seq + lax.axis_index("co")) * share
    share_ref[...] = raw[:, pl.ds(pl.multiple_of(place, 128), share)]


def set_up(levels, frames, block_mask, table_ref, bias_ref, gate_ref, held, sem):
    blocks, keys = bias_ref.shape
    rows, share = gate_ref.shape[0] // 2, gate_ref.shape[1]
    z, y, core = lax.axis_index("z"), lax.axis_index("y"), lax.axis_index("co")
    columns = pl.ds(pl.multiple_of((2 * lax.axis_index("xl") + core) * share, 128), share)
    level = levels[my_group()]
    aligned = pl.multiple_of((level // 8) * 8, 8)
    copy = pltpu.make_async_copy(table_ref.at[2, pl.ds(aligned, 8), columns], held, sem)
    copy.start()
    lane = lax.broadcasted_iota(jnp.int32, (1, keys), 1)
    for b in range(blocks):
        asker = z * NY + lax.rem(y + NY - b, NY)
        line = jnp.full((1, keys), HIDDEN, jnp.float32)
        for i in range(NZ):
            d = 0 if i == 0 else FAR[0][3]
            if 1 <= i <= 3:
                d = jnp.where(core == 0, FAR[0][i - 1], FAR[1][i - 1])
            elif 4 <= i <= 6:
                d = jnp.where(core == 0, FAR[1][i - 4], FAR[0][i - 4])
            block = lax.rem(z + NZ - d, NZ) * NY + y
            seen = (block == asker) | ((block < asker) & (block_mask[asker, block] == 1))
            count = jnp.where(seen, frames[block] * FT, 0)
            begin = i * (keys // NZ)
            line = jnp.where((lane >= begin) & (lane < begin + count), 0.0, line)
        bias_ref[pl.ds(b, 1), :] = line
    copy.wait()
    gate = held[pl.ds(lax.rem(level, 8), 1), :]
    row = lax.broadcasted_iota(jnp.int32, (rows, share), 0)
    for k in range(2):
        position = (lax.axis_index("xh") if k == 0 else 1 - lax.axis_index("xh")) * rows + row
        gate_ref[pl.ds(k * rows, rows), :] = jnp.where(position < frames[my_group()] * FT, gate, 0.0)


def terms_of(value, count):
    terms = []
    for _ in range(count):
        term = value.astype(jnp.bfloat16)
        terms.append(term)
        value = value - term.astype(jnp.float32)
    return terms


def project(tokens_ref, held, j, copies=None):
    depth = held.shape[1]
    steps = tokens_ref.shape[1] // depth
    total = None
    for i in range(steps):
        n = j * steps + i
        if copies is not None:
            copies[n].wait()
        part = tokens_ref[:, i * depth : (i + 1) * depth]
        term = jnp.dot(part, held[n], preferred_element_type=jnp.float32)
        total = term if total is None else total + term
    return total


def store_sums(out, *columns):
    rows, width = columns[0].shape
    for i, value in enumerate(columns):
        out[pl.ds(0, rows), pl.ds(i * width, width)] = value


def project_mine_kernel(tokens_ref, q_gain_in, k_gain_in, weight_ref, q_ref, kv_ref, held, q_gain_ref, k_gain_ref, sems):
    slots, depth, width = held.shape
    rows = tokens_ref.shape[0]
    small = [
        pltpu.make_async_copy(q_gain_in, q_gain_ref, sems.at[slots]),
        pltpu.make_async_copy(k_gain_in, k_gain_ref, sems.at[slots + 1]),
    ]
    for copy in small:
        copy.start()
    copies = []
    for n in range(slots):
        j, i = divmod(n, slots // 3)
        piece = weight_ref.at[j, pl.ds(i * depth, depth), :]
        copies.append(pltpu.make_async_copy(piece, held.at[n], sems.at[n]))
    for copy in copies:
        copy.start()
    for copy in small:
        copy.wait()
    gains = []
    for gain_ref in (k_gain_ref, q_gain_ref):
        gains += terms_of(gain_ref[...].reshape(1, width), 3)
    row = lax.broadcasted_iota(jnp.int32, (GAIN_ROWS, width), 0)
    for side in range(2):
        block = jnp.zeros((GAIN_ROWS, width), jnp.float32)
        for r in range(3):
            block = jnp.where(row == r, gains[2 * r + side].astype(jnp.float32), block)
        q_ref[pl.ds(rows, GAIN_ROWS), pl.ds(side * width, width)] = block.astype(jnp.bfloat16)
    store_sums(q_ref, *terms_of(project(tokens_ref, held, 0, copies), 2))
    key = project(tokens_ref, held, 1, copies)
    store_sums(kv_ref, *terms_of(key, 2), project(tokens_ref, held, 2, copies).astype(jnp.bfloat16))


def project_kv_kernel(got_ref, sib_ref, change_ref, share_ref, held, kv_ref, tokens_ref, rest_ref):
    share = share_ref.shape[1]
    core = lax.axis_index("co")
    terms = got_ref[:, pl.ds(share, STATS)].astype(jnp.float32)
    center = terms[:, 0:1] + terms[:, 1:2] + terms[:, 2:3]
    scale = terms[:, 3:4] + terms[:, 4:5] + terms[:, 5:6]
    for ref, at in ((got_ref, core), (sib_ref, 1 - core)):
        columns = pl.ds(pl.multiple_of(at * share, 128), share)
        centred = ref[:, pl.ds(0, share)].astype(jnp.float32) - center
        normed = centred * scale * change_ref[pl.ds(1, 1), columns] + change_ref[pl.ds(0, 1), columns]
        tokens_ref[:, columns] = normed.astype(jnp.bfloat16)
    other = got_ref[:, pl.ds(0, share)]
    rest_ref[...] = jnp.where(lax.axis_index("xh") == lax.axis_index("xl"), share_ref[...], other)
    key = project(tokens_ref, held, 1)
    store_sums(kv_ref, *terms_of(key, 2), project(tokens_ref, held, 2).astype(jnp.bfloat16))


def project_q_kernel(tokens_ref, held, q_ref):
    store_sums(q_ref, *terms_of(project(tokens_ref, held, 0), 2))


def head_norm(values, gain):
    square = jnp.mean(values * values, axis=-1, keepdims=True)
    return (values * lax.rsqrt(square + 1e-06) * gain).astype(jnp.bfloat16)


def wide(ref, *places):
    return sum(ref[place].astype(jnp.float32) for place in places)


def gain_of(which, q_ref, rows, h):
    width = q_ref.shape[1] // 2
    places = []
    for p in range(3 * which, 3 * which + 3):
        places.append((pl.ds(rows + p // 2, 1), pl.ds((p % 2) * width + h * HDIM, HDIM)))
    return wide(q_ref, *places)


def sum_of(a_ref, b_ref, rows, blocks, width, h):
    at = [(pl.ds(0, rows), pl.ds(i * width + h * HDIM, HDIM)) for i in blocks]
    return wide(a_ref, *at) + wide(b_ref, *at)


def kv_kernel(a_ref, b_ref, q_ref, waits_ref, out_ref):
    rows, width = out_ref.shape[0], out_ref.shape[1] // 2
    for h in range(width // HDIM):
        key = sum_of(a_ref, b_ref, rows, (0, 1), width, h)
        out_ref[:, pl.ds(h * HDIM, HDIM)] = head_norm(key, gain_of(0, q_ref, rows, h))
        value = sum_of(a_ref, b_ref, rows, (2,), width, h)
        out_ref[:, pl.ds(width + h * HDIM, HDIM)] = value.astype(jnp.bfloat16)


def query_kernel(levels, frames, block_mask, a_ref, b_ref, table_ref, waits_ref, out_ref, *rest):
    rows, width = out_ref.shape
    for h in range(width // HDIM):
        query = sum_of(a_ref, b_ref, rows, (0, 1), width, h)
        out_ref[:, pl.ds(h * HDIM, HDIM)] = head_norm(query, gain_of(1, a_ref, rows, h))
    set_up(levels, frames, block_mask, table_ref, *rest)


def chip_kernel(own_ref, sib_ref, waits_ref, out_ref):
    rows = own_ref.shape[0]
    core = lax.axis_index("co")
    out_ref[pl.ds(pl.multiple_of(core * rows, rows), rows), :] = own_ref[...]
    out_ref[pl.ds(pl.multiple_of((1 - core) * rows, rows), rows), :] = sib_ref[...]


def attention_kernel(*refs):
    asked_ref, own, came, beside, bias_ref, outs = refs[0], refs[1], refs[2:6], refs[6:10], refs[10], refs[-NY:]
    rows, width = asked_ref.shape[1:]
    keys_in = [own, *came[:3], *beside[:3]]
    y = lax.axis_index("y")
    asked = [asked_ref.at[lax.rem(y + NY - b, NY)] for b in range(NY)]
    first = lax.axis_index("co") == 0

    def rows_of(at):
        last = jnp.where(first, came[3][:, at], beside[3][:, at])
        return jnp.concatenate([r[:, at] for r in keys_in] + [last], axis=0)

    keys = bias_ref.shape[1]
    blocks = len(asked)
    bias = jnp.concatenate(
        [jnp.broadcast_to(bias_ref[b : b + 1, :], (rows, keys)) for b in range(blocks)], axis=0
    )
    stats = []
    for h in range(width // HDIM):
        at = pl.ds(h * HDIM, HDIM)
        past = pl.ds(width + h * HDIM, HDIM)
        q = jnp.concatenate([r[:, at] for r in asked], axis=0)
        k = rows_of(at)
        v = rows_of(past)
        scores = lax.dot_general(q, k, (((1,), (1,)), ((), ())), preferred_element_type=jnp.float32)
        scores = scores * (1.0 / math.sqrt(HDIM)) + bias
        top = jnp.max(scores, axis=1, keepdims=True).astype(jnp.bfloat16).astype(jnp.float32)
        weights = jnp.exp(scores - top)
        total = jnp.sum(weights, axis=1, keepdims=True)
        mixed = jnp.dot(weights.astype(jnp.bfloat16), v, preferred_element_type=jnp.float32)
        mixed = mixed.astype(jnp.bfloat16)
        for b, out in enumerate(outs):
            out[:, at] = mixed[b * rows : (b + 1) * rows]
        high = total.astype(jnp.bfloat16).astype(jnp.float32)
        stats += [top, high, total - high]
    lane = lax.broadcasted_iota(jnp.int32, (blocks * rows, STATS), 1)
    packed = jnp.zeros((blocks * rows, STATS), jnp.float32)
    for i, s in enumerate(stats):
        packed = jnp.where(lane == i, s, packed)
    packed = packed.astype(jnp.bfloat16)
    for b, out in enumerate(outs):
        out[:, pl.ds(width, STATS)] = packed[b * rows : (b + 1) * rows]


def merge_kernel(a_ref, b_ref, c_ref, d_ref, out_ref):
    width = out_ref.shape[1]
    parts = (a_ref, b_ref, c_ref, d_ref)
    stats = [p[:, pl.ds(width, STATS)].astype(jnp.float32) for p in parts]
    for h in range(width // HDIM):
        at = pl.ds(h * HDIM, HDIM)
        tops = [s[:, 3 * h : 3 * h + 1] for s in stats]
        sums = [s[:, 3 * h + 1 : 3 * h + 2] + s[:, 3 * h + 2 : 3 * h + 3] for s in stats]
        top = functools.reduce(jnp.maximum, tops)
        scales = [jnp.exp(t - top) for t in tops]
        total = sum(s * w for s, w in zip(sums, scales))
        mixed = sum(p[:, at].astype(jnp.float32) * w for p, w in zip(parts, scales))
        out_ref[:, at] = (mixed / total).astype(jnp.bfloat16)


def out_kernel(same_ref, other_ref, weight_ref, keep_ref, give_ref):
    rows, share = same_ref.shape[0], keep_ref.shape[1]
    swap = lax.axis_index("xl") != lax.axis_index("xh")
    same, other = same_ref[...], other_ref[...]
    tokens = jnp.concatenate([jnp.where(swap, other, same), jnp.where(swap, same, other)], axis=0)
    core = lax.axis_index("co")
    near = weight_ref[:, pl.ds(pl.multiple_of(core * share, 128), share)]
    give = weight_ref[:, pl.ds(pl.multiple_of((1 - core) * share, 128), share)]
    give_ref[...] = jnp.dot(tokens, give, preferred_element_type=jnp.float32).astype(jnp.bfloat16)
    keep_ref[...] = jnp.dot(tokens, near, preferred_element_type=jnp.float32)


def pieces_kernel(keep_ref, got_ref, gate_ref, rest_ref, first_ref, second_ref):
    rows = first_ref.shape[0]
    change = gate_ref[...] * (keep_ref[...] + got_ref[...].astype(jnp.float32))
    first_ref[...] = (rest_ref[...].astype(jnp.float32) + change[:rows]).astype(jnp.bfloat16)
    second_ref[...] = change[rows:].astype(jnp.bfloat16)


def per_device(
    stream, entering, qkv_weight, out_weight, q_gain, k_gain, mod_table, levels, frames, block_mask
):
    rows, model = stream.shape
    width = q_gain.shape[0]
    half, share = model // 2, model // 4
    keys = 2 * NZ * rows
    table = pltpu.with_memory_space_constraint(jnp.transpose(mod_table, (1, 0, 2)), pltpu.HBM)
    weight = pltpu.with_memory_space_constraint(jnp.transpose(qkv_weight, (1, 0, 2)), pltpu.HBM)

    mine, theirs, change, part = pl.pallas_call(
        norm_kernel,
        in_specs=[HBM, HBM, HBM],
        out_specs=[VMEM] * 4,
        out_shape=[
            like((rows, half)),
            like((rows, share + STATS)),
            like((2, half), jnp.float32),
            like((rows, share)),
        ],
        scratch_shapes=[
            pltpu.SMEM(levels.shape, jnp.int32),
            pltpu.VMEM((rows, model), jnp.bfloat16),
            pltpu.VMEM((2, 8, half), jnp.float32),
            pltpu.SemaphoreType.DMA((3,)),
        ],
        compiler_params=room(8),
        name="norm",
    )(
        pltpu.with_memory_space_constraint(levels, pltpu.HBM),
        pltpu.with_memory_space_constraint(stream, pltpu.HBM),
        table,
    )
    theirs = moved(theirs, ("xl",), lambda s: (1 - s,))

    slots = 12
    q_mine, kv_mine, kept = pl.pallas_call(
        project_mine_kernel,
        in_specs=[VMEM, HBM, HBM, HBM],
        out_specs=[VMEM] * 3,
        out_shape=[
            like((rows + GAIN_ROWS, 2 * width)),
            like((rows, 3 * width)),
            like((slots, 3 * half // slots, width)),
        ],
        scratch_shapes=[
            pltpu.VMEM((width,), jnp.float32),
            pltpu.VMEM((width,), jnp.float32),
            pltpu.SemaphoreType.DMA((slots + 2,)),
        ],
        compiler_params=room(16),
        name="project_mine",
    )(
        mine,
        pltpu.with_memory_space_constraint(q_gain, pltpu.HBM),
        pltpu.with_memory_space_constraint(k_gain, pltpu.HBM),
        weight,
    )
    theirs = after(theirs, kept)
    kv_mine = moved(kv_mine, ("xl", "co"), lambda s, c: (c, s))
    q_mine = moved(q_mine, ("xl", "co"), lambda s, c: (c, s))
    kv_got, got, rest = pl.pallas_call(
        project_kv_kernel,
        in_specs=[VMEM] * 5,
        out_specs=[VMEM] * 3,
        out_shape=[like((rows, 3 * width)), like((rows, half)), like((rows, share))],
        compiler_params=room(14),
        name="project_kv",
    )(theirs, moved(theirs, ("co",), lambda c: (1 - c,)), change, part, kept)
    kv_got = moved(kv_got, ("xl", "co"), lambda s, c: (c, 1 - s))
    q_got = pl.pallas_call(
        project_q_kernel,
        in_specs=[VMEM] * 2,
        out_specs=VMEM,
        out_shape=like((rows, 2 * width)),
        compiler_params=room(14),
        name="project_q",
    )(got, kept)
    pair = pl.pallas_call(
        kv_kernel,
        in_specs=[VMEM, VMEM, VMEM, ANY],
        out_specs=VMEM,
        out_shape=like((rows, 2 * width)),
        compiler_params=room(4),
        name="kv_heads",
    )(kv_mine, kv_got, q_mine, q_got)
    q_got = moved(q_got, ("xl", "co"), lambda s, c: (c, 1 - s))

    chip = pl.pallas_call(
        chip_kernel,
        in_specs=[VMEM, VMEM, ANY],
        out_specs=VMEM,
        out_shape=like((2 * rows, 2 * width)),
        compiler_params=room(4),
        name="chip",
    )(pair, moved(pair, ("co",), lambda c: (1 - c,)), q_got)

    def along(r):
        def target(a, c):
            return ((a + FAR[c][r]) % NZ, c) if r < len(FAR[c]) else None

        return target

    came = [moved(chip, ("z", "co"), along(r)) for r in range(len(FAR[0]))]

    queries, bias, gate = pl.pallas_call(
        query_kernel,
        in_specs=[SMEM, SMEM, SMEM, VMEM, VMEM, HBM, ANY],
        out_specs=[VMEM] * 3,
        out_shape=[
            like((rows, width)),
            like((NY, keys), jnp.float32),
            like((2 * rows, share), jnp.float32),
        ],
        scratch_shapes=[pltpu.VMEM((8, share), jnp.float32), pltpu.SemaphoreType.DMA],
        compiler_params=room(6),
        name="q_heads",
    )(levels, frames, block_mask, q_mine, q_got, table, chip)
    asked = lax.all_gather(queries, "y")
    came = [after(c, asked) for c in came]
    beside = [moved(c, ("co",), lambda c: (1 - c,)) for c in came]

    partial = pl.pallas_call(
        attention_kernel,
        in_specs=[VMEM] * 11,
        out_specs=[VMEM] * NY,
        out_shape=[like((rows, width + STATS))] * NY,
        compiler_params=room(16),
        name="attention",
    )(asked, chip, *came, *beside, bias)
    parts = [partial[0]]
    for d in range(1, NY):
        parts.append(moved(partial[d], ("y",), lambda b, d=d: ((b - d) % NY,)))
    attended = pl.pallas_call(
        merge_kernel, out_shape=like((rows, width)), compiler_params=room(4), name="merge"
    )(*parts)

    same = moved(attended, ("xl", "co"), lambda s, c: (c, s))
    other = moved(attended, ("xl", "co"), lambda s, c: (1 - c, s))
    keep, give = pl.pallas_call(
        out_kernel,
        in_specs=[VMEM, VMEM, VMEM],
        out_specs=[VMEM, VMEM],
        out_shape=[like((2 * rows, share), jnp.float32), like((2 * rows, share))],
        compiler_params=room(10),
        name="out",
    )(same, other, out_weight)
    first, second = pl.pallas_call(
        pieces_kernel,
        in_specs=[VMEM] * 4,
        out_specs=[VMEM] * 2,
        out_shape=[like((rows, share))] * 2,
        compiler_params=room(6),
        name="pieces",
    )(keep, moved(give, ("co",), lambda c: (1 - c,)), gate, rest)

    def onward(k):
        def target(a, b, s, h):
            goal = next_owner(a, b)
            return None if goal is None else goal + (k ^ h, s)

        return target

    first = moved(first, ("z", "y", "xl", "xh"), onward(0))
    second = moved(second, ("z", "y", "xl", "xh"), onward(1))
    updated = (first.astype(jnp.float32) + second.astype(jnp.float32)).astype(jnp.bfloat16)
    return jnp.where(my_group() == 0, entering, updated)


def solution(mesh):
    fine = Mesh(mesh.devices.reshape(SIZES), AXES)
    tensor = ("xh", "co")
    placed = (
        P(("z", "y", "xl"), None),
        P("xl", tensor),
        P("xl", None, tensor),
        P(tensor, "xl"),
        P(tensor),
        P(tensor),
        P(),
        P(),
        P(),
        P(),
    )
    return jax.shard_map(
        per_device,
        mesh=fine,
        in_specs=placed,
        out_specs=P(("z", "y", "xl"), tensor),
        check_vma=False,
    )
```

```python
import functools
import math

import jax
import jax.numpy as jnp
import numpy as np
from jax import lax
from jax.experimental import pallas as pl
from jax.experimental.pallas import tpu as pltpu
from jax.sharding import Mesh, PartitionSpec as P

HDIM = 128
FT = 32
AXES = ("z", "y", "xl", "xh", "co")
SIZES = (8, 4, 2, 2, 2)
NZ, NY = 8, 4
HIDDEN = -(2.0**100)
STATS = 128
GAIN_ROWS = 16
FAR = ((1, 7, 3), (2, 6, 5))
MIDDLE = NZ // 2
SMEM = pl.BlockSpec(memory_space=pltpu.SMEM)
VMEM = pl.BlockSpec(memory_space=pltpu.VMEM)
ANY = pl.BlockSpec(memory_space=pl.ANY)
HBM = pl.BlockSpec(memory_space=pltpu.HBM)


def room(mib):
    return pltpu.CompilerParams(vmem_limit_bytes=mib * 1024 * 1024)


def my_group():
    return lax.axis_index("z") * NY + lax.axis_index("y")


def like(shape, dtype=jnp.bfloat16):
    return jax.ShapeDtypeStruct(shape, dtype)


def moved(value, axes, target):
    sizes = [SIZES[AXES.index(axis)] for axis in axes]
    pairs = []
    for place in np.ndindex(*sizes):
        goal = target(*place)
        if goal is not None:
            pairs.append((int(np.ravel_multi_index(place, sizes)), int(np.ravel_multi_index(goal, sizes))))
    return lax.ppermute(value, axes, pairs)


def next_owner(z, y):
    goal = z * NY + y + 1
    return None if goal == NZ * NY else divmod(goal, NY)


def after(value, *others):
    return pl.pallas_call(
        lambda *refs: None,
        in_specs=[ANY] * (1 + len(others)),
        out_specs=ANY,
        out_shape=like(value.shape, value.dtype),
        input_output_aliases={0: 0},
        compiler_params=room(1),
        name="after",
    )(value, *others)


def norm_kernel(levels_ref, stream_ref, table_ref, mine_ref, theirs_ref, change_ref, share_ref, levels, raw, held, sems):
    rows, model = raw.shape
    half, share = mine_ref.shape[1], share_ref.shape[1]
    whole = pltpu.make_async_copy(stream_ref, raw, sems.at[0])
    whole.start()
    first = pltpu.make_async_copy(levels_ref, levels, sems.at[2])
    first.start()
    first.wait()
    level = levels[my_group()]
    begin = pl.multiple_of((level // 8) * 8, 8)
    seq = lax.axis_index("xl")
    columns = pl.ds(pl.multiple_of(seq * half, 128), half)
    copy = pltpu.make_async_copy(table_ref.at[pl.ds(0, 2), pl.ds(begin, 8), columns], held, sems.at[1])
    copy.start()
    whole.wait()
    values = raw[...].astype(jnp.float32)
    center = jnp.mean(values, axis=-1, keepdims=True)
    centred = values - center
    spread = jnp.mean(centred * centred, axis=-1, keepdims=True)
    scale = lax.rsqrt(spread + 1e-06)
    lane = lax.broadcasted_iota(jnp.int32, (rows, STATS), 1)
    terms = jnp.zeros((rows, STATS), jnp.float32)
    for i, left in enumerate((center, scale)):
        for j in range(3):
            term = left.astype(jnp.bfloat16).astype(jnp.float32)
            terms = jnp.where(lane == 3 * i + j, term, terms)
            left = left - term
    quarter = (1 - seq) * half + lax.axis_index("co") * share
    theirs_ref[:, pl.ds(0, share)] = raw[:, pl.ds(pl.multiple_of(quarter, 128), share)]
    theirs_ref[:, pl.ds(share, STATS)] = terms.astype(jnp.bfloat16)
    copy.wait()
    row = pl.ds(lax.rem(level, 8), 1)
    change_ref[pl.ds(0, 1), :] = held[0, row, :]
    change_ref[pl.ds(1, 1), :] = 1.0 + held[1, row, :]
    own = raw[:, columns].astype(jnp.float32)
    mine_ref[...] = ((own - center) * scale * change_ref[1:2, :] + change_ref[0:1, :]).astype(jnp.bfloat16)
    place = (2 * seq + lax.axis_index("co")) * share
    share_ref[...] = raw[:, pl.ds(pl.multiple_of(place, 128), share)]


def set_up(levels, frames, block_mask, table_ref, bias_ref, gate_ref, held, sem):
    blocks, keys = bias_ref.shape
    rows, share = gate_ref.shape[0] // 2, gate_ref.shape[1]
    z, y, core = lax.axis_index("z"), lax.axis_index("y"), lax.axis_index("co")
    columns = pl.ds(pl.multiple_of((2 * lax.axis_index("xl") + core) * share, 128), share)
    level = levels[my_group()]
    aligned = pl.multiple_of((level // 8) * 8, 8)
    copy = pltpu.make_async_copy(table_ref.at[2, pl.ds(aligned, 8), columns], held, sem)
    copy.start()
    lane = lax.broadcasted_iota(jnp.int32, (1, keys), 1)
    for b in range(blocks):
        asker = z * NY + lax.rem(y + NY - b, NY)
        line = jnp.full((1, keys), HIDDEN, jnp.float32)
        for i in range(NZ):
            d = 0 if i == 0 else MIDDLE
            if 1 <= i <= 3:
                d = jnp.where(core == 0, FAR[0][i - 1], FAR[1][i - 1])
            elif 4 <= i <= 6:
                d = jnp.where(core == 0, FAR[1][i - 4], FAR[0][i - 4])
            block = lax.rem(z + NZ - d, NZ) * NY + y
            seen = (block == asker) | ((block < asker) & (block_mask[asker, block] == 1))
            count = jnp.where(seen, frames[block] * FT, 0)
            begin = i * (keys // NZ)
            line = jnp.where((lane >= begin) & (lane < begin + count), 0.0, line)
        bias_ref[pl.ds(b, 1), :] = line
    copy.wait()
    gate = held[pl.ds(lax.rem(level, 8), 1), :]
    row = lax.broadcasted_iota(jnp.int32, (rows, share), 0)
    for k in range(2):
        position = (lax.axis_index("xh") if k == 0 else 1 - lax.axis_index("xh")) * rows + row
        gate_ref[pl.ds(k * rows, rows), :] = jnp.where(position < frames[my_group()] * FT, gate, 0.0)


def terms_of(value, count):
    terms = []
    for _ in range(count):
        term = value.astype(jnp.bfloat16)
        terms.append(term)
        value = value - term.astype(jnp.float32)
    return terms


def project(tokens_ref, held, j, copies=None):
    depth = held.shape[1]
    steps = tokens_ref.shape[1] // depth
    total = None
    for i in range(steps):
        n = j * steps + i
        if copies is not None:
            copies[n].wait()
        part = tokens_ref[:, i * depth : (i + 1) * depth]
        term = jnp.dot(part, held[n], preferred_element_type=jnp.float32)
        total = term if total is None else total + term
    return total


def store_sums(out, *columns):
    rows, width = columns[0].shape
    for i, value in enumerate(columns):
        out[pl.ds(0, rows), pl.ds(i * width, width)] = value


def project_mine_kernel(tokens_ref, q_gain_in, k_gain_in, weight_ref, q_ref, kv_ref, held, q_gain_ref, k_gain_ref, sems):
    slots, depth, width = held.shape
    rows = tokens_ref.shape[0]
    small = [
        pltpu.make_async_copy(q_gain_in, q_gain_ref, sems.at[slots]),
        pltpu.make_async_copy(k_gain_in, k_gain_ref, sems.at[slots + 1]),
    ]
    for copy in small:
        copy.start()
    copies = []
    for n in range(slots):
        j, i = divmod(n, slots // 3)
        piece = weight_ref.at[j, pl.ds(i * depth, depth), :]
        copies.append(pltpu.make_async_copy(piece, held.at[n], sems.at[n]))
    for copy in copies:
        copy.start()
    for copy in small:
        copy.wait()
    gains = []
    for gain_ref in (k_gain_ref, q_gain_ref):
        gains += terms_of(gain_ref[...].reshape(1, width), 3)
    row = lax.broadcasted_iota(jnp.int32, (GAIN_ROWS, width), 0)
    for side in range(2):
        block = jnp.zeros((GAIN_ROWS, width), jnp.float32)
        for r in range(3):
            block = jnp.where(row == r, gains[2 * r + side].astype(jnp.float32), block)
        q_ref[pl.ds(rows, GAIN_ROWS), pl.ds(side * width, width)] = block.astype(jnp.bfloat16)
    store_sums(q_ref, *terms_of(project(tokens_ref, held, 0, copies), 2))
    key = project(tokens_ref, held, 1, copies)
    store_sums(kv_ref, *terms_of(key, 2), project(tokens_ref, held, 2, copies).astype(jnp.bfloat16))


def project_kv_kernel(got_ref, sib_ref, change_ref, share_ref, held, kv_ref, tokens_ref, rest_ref):
    share = share_ref.shape[1]
    core = lax.axis_index("co")
    terms = got_ref[:, pl.ds(share, STATS)].astype(jnp.float32)
    center = terms[:, 0:1] + terms[:, 1:2] + terms[:, 2:3]
    scale = terms[:, 3:4] + terms[:, 4:5] + terms[:, 5:6]
    for ref, at in ((got_ref, core), (sib_ref, 1 - core)):
        columns = pl.ds(pl.multiple_of(at * share, 128), share)
        centred = ref[:, pl.ds(0, share)].astype(jnp.float32) - center
        normed = centred * scale * change_ref[pl.ds(1, 1), columns] + change_ref[pl.ds(0, 1), columns]
        tokens_ref[:, columns] = normed.astype(jnp.bfloat16)
    other = got_ref[:, pl.ds(0, share)]
    rest_ref[...] = jnp.where(lax.axis_index("xh") == lax.axis_index("xl"), share_ref[...], other)
    key = project(tokens_ref, held, 1)
    store_sums(kv_ref, *terms_of(key, 2), project(tokens_ref, held, 2).astype(jnp.bfloat16))


def project_q_kernel(tokens_ref, held, q_ref):
    store_sums(q_ref, *terms_of(project(tokens_ref, held, 0), 2))


def head_norm(values, gain):
    square = jnp.mean(values * values, axis=-1, keepdims=True)
    return (values * lax.rsqrt(square + 1e-06) * gain).astype(jnp.bfloat16)


def wide(ref, *places):
    return sum(ref[place].astype(jnp.float32) for place in places)


def gain_of(which, q_ref, rows, h):
    width = q_ref.shape[1] // 2
    places = []
    for p in range(3 * which, 3 * which + 3):
        places.append((pl.ds(rows + p // 2, 1), pl.ds((p % 2) * width + h * HDIM, HDIM)))
    return wide(q_ref, *places)


def sum_of(a_ref, b_ref, rows, blocks, width, h):
    at = [(pl.ds(0, rows), pl.ds(i * width + h * HDIM, HDIM)) for i in blocks]
    return wide(a_ref, *at) + wide(b_ref, *at)


def kv_kernel(a_ref, b_ref, q_ref, waits_ref, out_ref):
    rows, width = out_ref.shape[0], out_ref.shape[1] // 2
    for h in range(width // HDIM):
        key = sum_of(a_ref, b_ref, rows, (0, 1), width, h)
        out_ref[:, pl.ds(h * HDIM, HDIM)] = head_norm(key, gain_of(0, q_ref, rows, h))
        value = sum_of(a_ref, b_ref, rows, (2,), width, h)
        out_ref[:, pl.ds(width + h * HDIM, HDIM)] = value.astype(jnp.bfloat16)


def query_kernel(levels, frames, block_mask, a_ref, b_ref, table_ref, waits_ref, out_ref, *rest):
    rows, width = out_ref.shape
    for h in range(width // HDIM):
        query = sum_of(a_ref, b_ref, rows, (0, 1), width, h)
        out_ref[:, pl.ds(h * HDIM, HDIM)] = head_norm(query, gain_of(1, a_ref, rows, h))
    set_up(levels, frames, block_mask, table_ref, *rest)


def chip_kernel(own_ref, sib_ref, waits_ref, out_ref):
    rows = own_ref.shape[0]
    core = lax.axis_index("co")
    out_ref[pl.ds(pl.multiple_of(core * rows, rows), rows), :] = own_ref[...]
    out_ref[pl.ds(pl.multiple_of((1 - core) * rows, rows), rows), :] = sib_ref[...]


def attention_kernel(*refs):
    asked_ref, own, came, beside, bias_ref, outs = refs[0], refs[1], refs[2:6], refs[6:10], refs[10], refs[-NY:]
    rows, width = asked_ref.shape[1:]
    keys_in = [own, *came[:3], *beside[:3]]
    y = lax.axis_index("y")
    asked = [asked_ref.at[lax.rem(y + NY - b, NY)] for b in range(NY)]
    first = lax.axis_index("co") == 0

    def rows_of(at):
        own_half, other_half = came[3][:, at], beside[3][:, at]
        last = [jnp.where(first, own_half, other_half), jnp.where(first, other_half, own_half)]
        return jnp.concatenate([r[:, at] for r in keys_in] + last, axis=0)

    keys = bias_ref.shape[1]
    blocks = len(asked)
    bias = jnp.concatenate(
        [jnp.broadcast_to(bias_ref[b : b + 1, :], (rows, keys)) for b in range(blocks)], axis=0
    )
    stats = []
    for h in range(width // HDIM):
        at = pl.ds(h * HDIM, HDIM)
        past = pl.ds(width + h * HDIM, HDIM)
        q = jnp.concatenate([r[:, at] for r in asked], axis=0)
        k = rows_of(at)
        v = rows_of(past)
        scores = lax.dot_general(q, k, (((1,), (1,)), ((), ())), preferred_element_type=jnp.float32)
        scores = scores * (1.0 / math.sqrt(HDIM)) + bias
        top = jnp.max(scores, axis=1, keepdims=True).astype(jnp.bfloat16).astype(jnp.float32)
        weights = jnp.exp(scores - top)
        total = jnp.sum(weights, axis=1, keepdims=True)
        mixed = jnp.dot(weights.astype(jnp.bfloat16), v, preferred_element_type=jnp.float32)
        mixed = mixed.astype(jnp.bfloat16)
        for b, out in enumerate(outs):
            out[:, at] = mixed[b * rows : (b + 1) * rows]
        high = total.astype(jnp.bfloat16).astype(jnp.float32)
        stats += [top, high, total - high]
    lane = lax.broadcasted_iota(jnp.int32, (blocks * rows, STATS), 1)
    packed = jnp.zeros((blocks * rows, STATS), jnp.float32)
    for i, s in enumerate(stats):
        packed = jnp.where(lane == i, s, packed)
    packed = packed.astype(jnp.bfloat16)
    for b, out in enumerate(outs):
        out[:, pl.ds(width, STATS)] = packed[b * rows : (b + 1) * rows]


def merge_kernel(a_ref, b_ref, c_ref, d_ref, out_ref):
    width = out_ref.shape[1]
    parts = (a_ref, b_ref, c_ref, d_ref)
    stats = [p[:, pl.ds(width, STATS)].astype(jnp.float32) for p in parts]
    for h in range(width // HDIM):
        at = pl.ds(h * HDIM, HDIM)
        tops = [s[:, 3 * h : 3 * h + 1] for s in stats]
        sums = [s[:, 3 * h + 1 : 3 * h + 2] + s[:, 3 * h + 2 : 3 * h + 3] for s in stats]
        top = functools.reduce(jnp.maximum, tops)
        scales = [jnp.exp(t - top) for t in tops]
        total = sum(s * w for s, w in zip(sums, scales))
        mixed = sum(p[:, at].astype(jnp.float32) * w for p, w in zip(parts, scales))
        out_ref[:, at] = (mixed / total).astype(jnp.bfloat16)


def out_kernel(same_ref, other_ref, weight_ref, keep_ref, give_ref):
    rows, share = same_ref.shape[0], keep_ref.shape[1]
    swap = lax.axis_index("xl") != lax.axis_index("xh")
    same, other = same_ref[...], other_ref[...]
    tokens = jnp.concatenate([jnp.where(swap, other, same), jnp.where(swap, same, other)], axis=0)
    core = lax.axis_index("co")
    near = weight_ref[:, pl.ds(pl.multiple_of(core * share, 128), share)]
    give = weight_ref[:, pl.ds(pl.multiple_of((1 - core) * share, 128), share)]
    give_ref[...] = jnp.dot(tokens, give, preferred_element_type=jnp.float32).astype(jnp.bfloat16)
    keep_ref[...] = jnp.dot(tokens, near, preferred_element_type=jnp.float32)


def pieces_kernel(keep_ref, got_ref, gate_ref, rest_ref, first_ref, second_ref):
    rows = first_ref.shape[0]
    change = gate_ref[...] * (keep_ref[...] + got_ref[...].astype(jnp.float32))
    first_ref[...] = (rest_ref[...].astype(jnp.float32) + change[:rows]).astype(jnp.bfloat16)
    second_ref[...] = change[rows:].astype(jnp.bfloat16)


def per_device(
    stream, entering, qkv_weight, out_weight, q_gain, k_gain, mod_table, levels, frames, block_mask
):
    rows, model = stream.shape
    width = q_gain.shape[0]
    half, share = model // 2, model // 4
    keys = 2 * NZ * rows
    table = pltpu.with_memory_space_constraint(jnp.transpose(mod_table, (1, 0, 2)), pltpu.HBM)
    weight = pltpu.with_memory_space_constraint(jnp.transpose(qkv_weight, (1, 0, 2)), pltpu.HBM)

    mine, theirs, change, part = pl.pallas_call(
        norm_kernel,
        in_specs=[HBM, HBM, HBM],
        out_specs=[VMEM] * 4,
        out_shape=[
            like((rows, half)),
            like((rows, share + STATS)),
            like((2, half), jnp.float32),
            like((rows, share)),
        ],
        scratch_shapes=[
            pltpu.SMEM(levels.shape, jnp.int32),
            pltpu.VMEM((rows, model), jnp.bfloat16),
            pltpu.VMEM((2, 8, half), jnp.float32),
            pltpu.SemaphoreType.DMA((3,)),
        ],
        compiler_params=room(8),
        name="norm",
    )(
        pltpu.with_memory_space_constraint(levels, pltpu.HBM),
        pltpu.with_memory_space_constraint(stream, pltpu.HBM),
        table,
    )
    theirs = moved(theirs, ("xl",), lambda s: (1 - s,))

    slots = 12
    q_mine, kv_mine, kept = pl.pallas_call(
        project_mine_kernel,
        in_specs=[VMEM, HBM, HBM, HBM],
        out_specs=[VMEM] * 3,
        out_shape=[
            like((rows + GAIN_ROWS, 2 * width)),
            like((rows, 3 * width)),
            like((slots, 3 * half // slots, width)),
        ],
        scratch_shapes=[
            pltpu.VMEM((width,), jnp.float32),
            pltpu.VMEM((width,), jnp.float32),
            pltpu.SemaphoreType.DMA((slots + 2,)),
        ],
        compiler_params=room(16),
        name="project_mine",
    )(
        mine,
        pltpu.with_memory_space_constraint(q_gain, pltpu.HBM),
        pltpu.with_memory_space_constraint(k_gain, pltpu.HBM),
        weight,
    )
    theirs = after(theirs, kept)
    kv_mine = moved(kv_mine, ("xl", "co"), lambda s, c: (c, s))
    q_mine = moved(q_mine, ("xl", "co"), lambda s, c: (c, s))
    kv_got, got, rest = pl.pallas_call(
        project_kv_kernel,
        in_specs=[VMEM] * 5,
        out_specs=[VMEM] * 3,
        out_shape=[like((rows, 3 * width)), like((rows, half)), like((rows, share))],
        compiler_params=room(14),
        name="project_kv",
    )(theirs, moved(theirs, ("co",), lambda c: (1 - c,)), change, part, kept)
    kv_got = moved(kv_got, ("xl", "co"), lambda s, c: (c, 1 - s))
    q_got = pl.pallas_call(
        project_q_kernel,
        in_specs=[VMEM] * 2,
        out_specs=VMEM,
        out_shape=like((rows, 2 * width)),
        compiler_params=room(14),
        name="project_q",
    )(got, kept)
    pair = pl.pallas_call(
        kv_kernel,
        in_specs=[VMEM, VMEM, VMEM, ANY],
        out_specs=VMEM,
        out_shape=like((rows, 2 * width)),
        compiler_params=room(4),
        name="kv_heads",
    )(kv_mine, kv_got, q_mine, q_got)
    q_got = moved(q_got, ("xl", "co"), lambda s, c: (c, 1 - s))

    chip = pl.pallas_call(
        chip_kernel,
        in_specs=[VMEM, VMEM, ANY],
        out_specs=VMEM,
        out_shape=like((2 * rows, 2 * width)),
        compiler_params=room(4),
        name="chip",
    )(pair, moved(pair, ("co",), lambda c: (1 - c,)), q_got)

    def along(r):
        def target(a, c):
            return (a + FAR[c][r]) % NZ, c

        return target

    came = [moved(chip, ("z", "co"), along(r)) for r in range(len(FAR[0]))]
    came.append(moved(pair, ("z",), lambda a: ((a + MIDDLE) % NZ,)))

    queries, bias, gate = pl.pallas_call(
        query_kernel,
        in_specs=[SMEM, SMEM, SMEM, VMEM, VMEM, HBM, ANY],
        out_specs=[VMEM] * 3,
        out_shape=[
            like((rows, width)),
            like((NY, keys), jnp.float32),
            like((2 * rows, share), jnp.float32),
        ],
        scratch_shapes=[pltpu.VMEM((8, share), jnp.float32), pltpu.SemaphoreType.DMA],
        compiler_params=room(6),
        name="q_heads",
    )(levels, frames, block_mask, q_mine, q_got, table, chip)
    asked = lax.all_gather(queries, "y")
    came = [after(c, asked) for c in came]
    beside = [moved(c, ("co",), lambda c: (1 - c,)) for c in came]

    partial = pl.pallas_call(
        attention_kernel,
        in_specs=[VMEM] * 11,
        out_specs=[VMEM] * NY,
        out_shape=[like((rows, width + STATS))] * NY,
        compiler_params=room(16),
        name="attention",
    )(asked, chip, *came, *beside, bias)
    parts = [partial[0]]
    for d in range(1, NY):
        parts.append(moved(partial[d], ("y",), lambda b, d=d: ((b - d) % NY,)))
    attended = pl.pallas_call(
        merge_kernel, out_shape=like((rows, width)), compiler_params=room(4), name="merge"
    )(*parts)

    same = moved(attended, ("xl", "co"), lambda s, c: (c, s))
    other = moved(attended, ("xl", "co"), lambda s, c: (1 - c, s))
    keep, give = pl.pallas_call(
        out_kernel,
        in_specs=[VMEM, VMEM, VMEM],
        out_specs=[VMEM, VMEM],
        out_shape=[like((2 * rows, share), jnp.float32), like((2 * rows, share))],
        compiler_params=room(10),
        name="out",
    )(same, other, out_weight)
    first, second = pl.pallas_call(
        pieces_kernel,
        in_specs=[VMEM] * 4,
        out_specs=[VMEM] * 2,
        out_shape=[like((rows, share))] * 2,
        compiler_params=room(6),
        name="pieces",
    )(keep, moved(give, ("co",), lambda c: (1 - c,)), gate, rest)

    def onward(k):
        def target(a, b, s, h):
            goal = next_owner(a, b)
            return None if goal is None else goal + (k ^ h, s)

        return target

    first = moved(first, ("z", "y", "xl", "xh"), onward(0))
    second = moved(second, ("z", "y", "xl", "xh"), onward(1))
    updated = (first.astype(jnp.float32) + second.astype(jnp.float32)).astype(jnp.bfloat16)
    return jnp.where(my_group() == 0, entering, updated)


def solution(mesh):
    fine = Mesh(mesh.devices.reshape(SIZES), AXES)
    tensor = ("xh", "co")
    placed = (
        P(("z", "y", "xl"), None),
        P("xl", tensor),
        P("xl", None, tensor),
        P(tensor, "xl"),
        P(tensor),
        P(tensor),
        P(),
        P(),
        P(),
        P(),
    )
    return jax.shard_map(
        per_device,
        mesh=fine,
        in_specs=placed,
        out_specs=P(("z", "y", "xl"), tensor),
        check_vma=False,
    )
```

```python
import functools
import math

import jax
import jax.numpy as jnp
import numpy as np
from jax import lax
from jax.experimental import pallas as pl
from jax.experimental.pallas import tpu as pltpu
from jax.sharding import Mesh, PartitionSpec as P

HDIM = 128
FT = 32
AXES = ("z", "y", "xl", "xh", "co")
SIZES = (8, 4, 2, 2, 2)
NZ, NY = 8, 4
HIDDEN = -(2.0**100)
STATS = 128
GAIN_ROWS = 16
FAR = ((1, 7, 3), (2, 6, 5))
MIDDLE = NZ // 2
SMEM = pl.BlockSpec(memory_space=pltpu.SMEM)
VMEM = pl.BlockSpec(memory_space=pltpu.VMEM)
ANY = pl.BlockSpec(memory_space=pl.ANY)
HBM = pl.BlockSpec(memory_space=pltpu.HBM)


def room(mib):
    return pltpu.CompilerParams(vmem_limit_bytes=mib * 1024 * 1024)


def my_group():
    return lax.axis_index("z") * NY + lax.axis_index("y")


def like(shape, dtype=jnp.bfloat16):
    return jax.ShapeDtypeStruct(shape, dtype)


def moved(value, axes, target):
    sizes = [SIZES[AXES.index(axis)] for axis in axes]
    pairs = []
    for place in np.ndindex(*sizes):
        goal = target(*place)
        if goal is not None:
            pairs.append((int(np.ravel_multi_index(place, sizes)), int(np.ravel_multi_index(goal, sizes))))
    return lax.ppermute(value, axes, pairs)


def next_owner(z, y):
    goal = z * NY + y + 1
    return None if goal == NZ * NY else divmod(goal, NY)


def after(value, *others):
    return pl.pallas_call(
        lambda *refs: None,
        in_specs=[ANY] * (1 + len(others)),
        out_specs=ANY,
        out_shape=like(value.shape, value.dtype),
        input_output_aliases={0: 0},
        compiler_params=room(1),
        name="after",
    )(value, *others)


def norm_kernel(levels_ref, stream_ref, table_ref, mine_ref, theirs_ref, change_ref, share_ref, levels, raw, held, sems):
    rows, model = raw.shape
    half, share = mine_ref.shape[1], share_ref.shape[1]
    whole = pltpu.make_async_copy(stream_ref, raw, sems.at[0])
    whole.start()
    first = pltpu.make_async_copy(levels_ref, levels, sems.at[2])
    first.start()
    first.wait()
    level = levels[my_group()]
    begin = pl.multiple_of((level // 8) * 8, 8)
    seq = lax.axis_index("xl")
    columns = pl.ds(pl.multiple_of(seq * half, 128), half)
    copy = pltpu.make_async_copy(table_ref.at[pl.ds(0, 2), pl.ds(begin, 8), columns], held, sems.at[1])
    copy.start()
    whole.wait()
    values = raw[...].astype(jnp.float32)
    center = jnp.mean(values, axis=-1, keepdims=True)
    centred = values - center
    spread = jnp.mean(centred * centred, axis=-1, keepdims=True)
    scale = lax.rsqrt(spread + 1e-06)
    lane = lax.broadcasted_iota(jnp.int32, (rows, STATS), 1)
    terms = jnp.zeros((rows, STATS), jnp.float32)
    for i, left in enumerate((center, scale)):
        for j in range(3):
            term = left.astype(jnp.bfloat16).astype(jnp.float32)
            terms = jnp.where(lane == 3 * i + j, term, terms)
            left = left - term
    quarter = (1 - seq) * half + lax.axis_index("co") * share
    theirs_ref[:, pl.ds(0, share)] = raw[:, pl.ds(pl.multiple_of(quarter, 128), share)]
    theirs_ref[:, pl.ds(share, STATS)] = terms.astype(jnp.bfloat16)
    copy.wait()
    row = pl.ds(lax.rem(level, 8), 1)
    change_ref[pl.ds(0, 1), :] = held[0, row, :]
    change_ref[pl.ds(1, 1), :] = 1.0 + held[1, row, :]
    own = raw[:, columns].astype(jnp.float32)
    mine_ref[...] = ((own - center) * scale * change_ref[1:2, :] + change_ref[0:1, :]).astype(jnp.bfloat16)
    place = (2 * seq + lax.axis_index("co")) * share
    share_ref[...] = raw[:, pl.ds(pl.multiple_of(place, 128), share)]


def set_up(levels, frames, block_mask, table_ref, bias_ref, gate_ref, held, sem):
    blocks, keys = bias_ref.shape
    rows, share = gate_ref.shape[0] // 2, gate_ref.shape[1]
    z, y, core = lax.axis_index("z"), lax.axis_index("y"), lax.axis_index("co")
    columns = pl.ds(pl.multiple_of((2 * lax.axis_index("xl") + core) * share, 128), share)
    level = levels[my_group()]
    aligned = pl.multiple_of((level // 8) * 8, 8)
    copy = pltpu.make_async_copy(table_ref.at[2, pl.ds(aligned, 8), columns], held, sem)
    copy.start()
    lane = lax.broadcasted_iota(jnp.int32, (1, keys), 1)
    for b in range(blocks):
        asker = z * NY + lax.rem(y + NY - b, NY)
        line = jnp.full((1, keys), HIDDEN, jnp.float32)
        for i in range(NZ):
            d = 0 if i == 0 else MIDDLE
            if 1 <= i <= 3:
                d = jnp.where(core == 0, FAR[0][i - 1], FAR[1][i - 1])
            elif 4 <= i <= 6:
                d = jnp.where(core == 0, FAR[1][i - 4], FAR[0][i - 4])
            block = lax.rem(z + NZ - d, NZ) * NY + y
            seen = (block == asker) | ((block < asker) & (block_mask[asker, block] == 1))
            count = jnp.where(seen, frames[block] * FT, 0)
            begin = i * (keys // NZ)
            line = jnp.where((lane >= begin) & (lane < begin + count), 0.0, line)
        bias_ref[pl.ds(b, 1), :] = line
    copy.wait()
    gate = held[pl.ds(lax.rem(level, 8), 1), :]
    row = lax.broadcasted_iota(jnp.int32, (rows, share), 0)
    for k in range(2):
        position = (lax.axis_index("xh") if k == 0 else 1 - lax.axis_index("xh")) * rows + row
        gate_ref[pl.ds(k * rows, rows), :] = jnp.where(position < frames[my_group()] * FT, gate, 0.0)


def terms_of(value, count):
    terms = []
    for _ in range(count):
        term = value.astype(jnp.bfloat16)
        terms.append(term)
        value = value - term.astype(jnp.float32)
    return terms


def project(tokens_ref, held, j, copies=None):
    depth = held.shape[1]
    steps = tokens_ref.shape[1] // depth
    total = None
    for i in range(steps):
        n = j * steps + i
        if copies is not None:
            copies[n].wait()
        part = tokens_ref[:, i * depth : (i + 1) * depth]
        term = jnp.dot(part, held[n], preferred_element_type=jnp.float32)
        total = term if total is None else total + term
    return total


def store_sums(out, *columns):
    rows, width = columns[0].shape
    for i, value in enumerate(columns):
        out[pl.ds(0, rows), pl.ds(i * width, width)] = value


def project_mine_kernel(tokens_ref, q_gain_in, k_gain_in, weight_ref, q_ref, kv_ref, held, q_gain_ref, k_gain_ref, sems):
    slots, depth, width = held.shape
    rows = tokens_ref.shape[0]
    small = [
        pltpu.make_async_copy(q_gain_in, q_gain_ref, sems.at[slots]),
        pltpu.make_async_copy(k_gain_in, k_gain_ref, sems.at[slots + 1]),
    ]
    for copy in small:
        copy.start()
    copies = []
    for n in range(slots):
        j, i = divmod(n, slots // 3)
        piece = weight_ref.at[j, pl.ds(i * depth, depth), :]
        copies.append(pltpu.make_async_copy(piece, held.at[n], sems.at[n]))
    for copy in copies:
        copy.start()
    for copy in small:
        copy.wait()
    gains = []
    for gain_ref in (k_gain_ref, q_gain_ref):
        gains += terms_of(gain_ref[...].reshape(1, width), 3)
    row = lax.broadcasted_iota(jnp.int32, (GAIN_ROWS, width), 0)
    for side in range(2):
        block = jnp.zeros((GAIN_ROWS, width), jnp.float32)
        for r in range(3):
            block = jnp.where(row == r, gains[2 * r + side].astype(jnp.float32), block)
        q_ref[pl.ds(rows, GAIN_ROWS), pl.ds(side * width, width)] = block.astype(jnp.bfloat16)
    store_sums(q_ref, *terms_of(project(tokens_ref, held, 0, copies), 2))
    key = project(tokens_ref, held, 1, copies)
    store_sums(kv_ref, *terms_of(key, 2), project(tokens_ref, held, 2, copies).astype(jnp.bfloat16))


def project_kv_kernel(got_ref, sib_ref, change_ref, share_ref, held, kv_ref, tokens_ref, rest_ref):
    share = share_ref.shape[1]
    core = lax.axis_index("co")
    terms = got_ref[:, pl.ds(share, STATS)].astype(jnp.float32)
    center = terms[:, 0:1] + terms[:, 1:2] + terms[:, 2:3]
    scale = terms[:, 3:4] + terms[:, 4:5] + terms[:, 5:6]
    for ref, at in ((got_ref, core), (sib_ref, 1 - core)):
        columns = pl.ds(pl.multiple_of(at * share, 128), share)
        centred = ref[:, pl.ds(0, share)].astype(jnp.float32) - center
        normed = centred * scale * change_ref[pl.ds(1, 1), columns] + change_ref[pl.ds(0, 1), columns]
        tokens_ref[:, columns] = normed.astype(jnp.bfloat16)
    other = got_ref[:, pl.ds(0, share)]
    rest_ref[...] = jnp.where(lax.axis_index("xh") == lax.axis_index("xl"), share_ref[...], other)
    key = project(tokens_ref, held, 1)
    store_sums(kv_ref, *terms_of(key, 2), project(tokens_ref, held, 2).astype(jnp.bfloat16))


def project_q_kernel(tokens_ref, held, q_ref):
    store_sums(q_ref, *terms_of(project(tokens_ref, held, 0), 2))


def head_norm(values, gain):
    square = jnp.mean(values * values, axis=-1, keepdims=True)
    return (values * lax.rsqrt(square + 1e-06) * gain).astype(jnp.bfloat16)


def wide(ref, *places):
    return sum(ref[place].astype(jnp.float32) for place in places)


def gain_of(which, q_ref, rows, h):
    width = q_ref.shape[1] // 2
    gain = 0.0
    for p in range(3 * which, 3 * which + 3):
        columns = pl.ds((p % 2) * width + h * HDIM, HDIM)
        block = q_ref[pl.ds(rows, GAIN_ROWS), columns].astype(jnp.float32)
        gain = gain + block[p // 2 : p // 2 + 1]
    return gain


def sum_of(a_ref, b_ref, rows, blocks, width, h):
    at = [(pl.ds(0, rows), pl.ds(i * width + h * HDIM, HDIM)) for i in blocks]
    return wide(a_ref, *at) + wide(b_ref, *at)


def kv_kernel(a_ref, b_ref, q_ref, waits_ref, out_ref):
    rows, width = out_ref.shape[0], out_ref.shape[1] // 2
    for h in range(width // HDIM):
        key = sum_of(a_ref, b_ref, rows, (0, 1), width, h)
        out_ref[:, pl.ds(h * HDIM, HDIM)] = head_norm(key, gain_of(0, q_ref, rows, h))
        value = sum_of(a_ref, b_ref, rows, (2,), width, h)
        out_ref[:, pl.ds(width + h * HDIM, HDIM)] = value.astype(jnp.bfloat16)


def query_kernel(levels, frames, block_mask, a_ref, b_ref, table_ref, waits_ref, out_ref, *rest):
    rows, width = out_ref.shape
    for h in range(width // HDIM):
        query = sum_of(a_ref, b_ref, rows, (0, 1), width, h)
        out_ref[:, pl.ds(h * HDIM, HDIM)] = head_norm(query, gain_of(1, a_ref, rows, h))
    set_up(levels, frames, block_mask, table_ref, *rest)


def chip_kernel(own_ref, sib_ref, waits_ref, out_ref):
    rows = own_ref.shape[0]
    core = lax.axis_index("co")
    out_ref[pl.ds(pl.multiple_of(core * rows, rows), rows), :] = own_ref[...]
    out_ref[pl.ds(pl.multiple_of((1 - core) * rows, rows), rows), :] = sib_ref[...]


def attention_kernel(*refs):
    asked_ref, own, came, beside, bias_ref, outs = refs[0], refs[1], refs[2:6], refs[6:10], refs[10], refs[-NY:]
    rows, width = asked_ref.shape[1:]
    keys_in = [own, *came[:3], *beside[:3]]
    y = lax.axis_index("y")
    asked = [asked_ref.at[lax.rem(y + NY - b, NY)] for b in range(NY)]
    first = lax.axis_index("co") == 0

    def rows_of(at):
        own_half, other_half = came[3][:, at], beside[3][:, at]
        last = [jnp.where(first, own_half, other_half), jnp.where(first, other_half, own_half)]
        return jnp.concatenate([r[:, at] for r in keys_in] + last, axis=0)

    keys = bias_ref.shape[1]
    blocks = len(asked)
    bias = jnp.concatenate(
        [jnp.broadcast_to(bias_ref[b : b + 1, :], (rows, keys)) for b in range(blocks)], axis=0
    )
    stats = []
    for h in range(width // HDIM):
        at = pl.ds(h * HDIM, HDIM)
        past = pl.ds(width + h * HDIM, HDIM)
        q = jnp.concatenate([r[:, at] for r in asked], axis=0)
        k = rows_of(at)
        v = rows_of(past)
        scores = lax.dot_general(q, k, (((1,), (1,)), ((), ())), preferred_element_type=jnp.float32)
        scores = scores * (1.0 / math.sqrt(HDIM)) + bias
        top = jnp.max(scores, axis=1, keepdims=True).astype(jnp.bfloat16).astype(jnp.float32)
        weights = jnp.exp(scores - top)
        total = jnp.sum(weights, axis=1, keepdims=True)
        mixed = jnp.dot(weights.astype(jnp.bfloat16), v, preferred_element_type=jnp.float32)
        mixed = mixed.astype(jnp.bfloat16)
        for b, out in enumerate(outs):
            out[:, at] = mixed[b * rows : (b + 1) * rows]
        high = total.astype(jnp.bfloat16).astype(jnp.float32)
        stats += [top, high, total - high]
    lane = lax.broadcasted_iota(jnp.int32, (blocks * rows, STATS), 1)
    packed = jnp.zeros((blocks * rows, STATS), jnp.float32)
    for i, s in enumerate(stats):
        packed = jnp.where(lane == i, s, packed)
    packed = packed.astype(jnp.bfloat16)
    for b, out in enumerate(outs):
        out[:, pl.ds(width, STATS)] = packed[b * rows : (b + 1) * rows]


def merge_kernel(a_ref, b_ref, c_ref, d_ref, out_ref):
    width = out_ref.shape[1]
    parts = (a_ref, b_ref, c_ref, d_ref)
    stats = [p[:, pl.ds(width, STATS)].astype(jnp.float32) for p in parts]
    for h in range(width // HDIM):
        at = pl.ds(h * HDIM, HDIM)
        tops = [s[:, 3 * h : 3 * h + 1] for s in stats]
        sums = [s[:, 3 * h + 1 : 3 * h + 2] + s[:, 3 * h + 2 : 3 * h + 3] for s in stats]
        top = functools.reduce(jnp.maximum, tops)
        scales = [jnp.exp(t - top) for t in tops]
        total = sum(s * w for s, w in zip(sums, scales))
        mixed = sum(p[:, at].astype(jnp.float32) * w for p, w in zip(parts, scales))
        out_ref[:, at] = (mixed / total).astype(jnp.bfloat16)


def out_kernel(same_ref, other_ref, weight_ref, keep_ref, give_ref):
    rows, share = same_ref.shape[0], keep_ref.shape[1]
    swap = lax.axis_index("xl") != lax.axis_index("xh")
    same, other = same_ref[...], other_ref[...]
    tokens = jnp.concatenate([jnp.where(swap, other, same), jnp.where(swap, same, other)], axis=0)
    core = lax.axis_index("co")
    near = weight_ref[:, pl.ds(pl.multiple_of(core * share, 128), share)]
    give = weight_ref[:, pl.ds(pl.multiple_of((1 - core) * share, 128), share)]
    give_ref[...] = jnp.dot(tokens, give, preferred_element_type=jnp.float32).astype(jnp.bfloat16)
    keep_ref[...] = jnp.dot(tokens, near, preferred_element_type=jnp.float32)


def pieces_kernel(keep_ref, got_ref, gate_ref, rest_ref, first_ref, second_ref):
    rows = first_ref.shape[0]
    change = gate_ref[...] * (keep_ref[...] + got_ref[...].astype(jnp.float32))
    first_ref[...] = (rest_ref[...].astype(jnp.float32) + change[:rows]).astype(jnp.bfloat16)
    second_ref[...] = change[rows:].astype(jnp.bfloat16)


def per_device(
    stream, entering, qkv_weight, out_weight, q_gain, k_gain, mod_table, levels, frames, block_mask
):
    rows, model = stream.shape
    width = q_gain.shape[0]
    half, share = model // 2, model // 4
    keys = 2 * NZ * rows
    table = pltpu.with_memory_space_constraint(jnp.transpose(mod_table, (1, 0, 2)), pltpu.HBM)
    weight = pltpu.with_memory_space_constraint(jnp.transpose(qkv_weight, (1, 0, 2)), pltpu.HBM)

    mine, theirs, change, part = pl.pallas_call(
        norm_kernel,
        in_specs=[HBM, HBM, HBM],
        out_specs=[VMEM] * 4,
        out_shape=[
            like((rows, half)),
            like((rows, share + STATS)),
            like((2, half), jnp.float32),
            like((rows, share)),
        ],
        scratch_shapes=[
            pltpu.SMEM(levels.shape, jnp.int32),
            pltpu.VMEM((rows, model), jnp.bfloat16),
            pltpu.VMEM((2, 8, half), jnp.float32),
            pltpu.SemaphoreType.DMA((3,)),
        ],
        compiler_params=room(8),
        name="norm",
    )(
        pltpu.with_memory_space_constraint(levels, pltpu.HBM),
        pltpu.with_memory_space_constraint(stream, pltpu.HBM),
        table,
    )
    theirs = moved(theirs, ("xl",), lambda s: (1 - s,))

    slots = 12
    q_mine, kv_mine, kept = pl.pallas_call(
        project_mine_kernel,
        in_specs=[VMEM, HBM, HBM, HBM],
        out_specs=[VMEM] * 3,
        out_shape=[
            like((rows + GAIN_ROWS, 2 * width)),
            like((rows, 3 * width)),
            like((slots, 3 * half // slots, width)),
        ],
        scratch_shapes=[
            pltpu.VMEM((width,), jnp.float32),
            pltpu.VMEM((width,), jnp.float32),
            pltpu.SemaphoreType.DMA((slots + 2,)),
        ],
        compiler_params=room(16),
        name="project_mine",
    )(
        mine,
        pltpu.with_memory_space_constraint(q_gain, pltpu.HBM),
        pltpu.with_memory_space_constraint(k_gain, pltpu.HBM),
        weight,
    )
    theirs = after(theirs, kept)
    kv_mine = moved(kv_mine, ("xl", "co"), lambda s, c: (c, s))
    q_mine = moved(q_mine, ("xl", "co"), lambda s, c: (c, s))
    kv_got, got, rest = pl.pallas_call(
        project_kv_kernel,
        in_specs=[VMEM] * 5,
        out_specs=[VMEM] * 3,
        out_shape=[like((rows, 3 * width)), like((rows, half)), like((rows, share))],
        compiler_params=room(14),
        name="project_kv",
    )(theirs, moved(theirs, ("co",), lambda c: (1 - c,)), change, part, kept)
    kv_got = moved(kv_got, ("xl", "co"), lambda s, c: (c, 1 - s))
    q_got = pl.pallas_call(
        project_q_kernel,
        in_specs=[VMEM] * 2,
        out_specs=VMEM,
        out_shape=like((rows, 2 * width)),
        compiler_params=room(14),
        name="project_q",
    )(got, kept)
    pair = pl.pallas_call(
        kv_kernel,
        in_specs=[VMEM, VMEM, VMEM, ANY],
        out_specs=VMEM,
        out_shape=like((rows, 2 * width)),
        compiler_params=room(4),
        name="kv_heads",
    )(kv_mine, kv_got, q_mine, q_got)
    q_got = moved(q_got, ("xl", "co"), lambda s, c: (c, 1 - s))

    chip = pl.pallas_call(
        chip_kernel,
        in_specs=[VMEM, VMEM, ANY],
        out_specs=VMEM,
        out_shape=like((2 * rows, 2 * width)),
        compiler_params=room(4),
        name="chip",
    )(pair, moved(pair, ("co",), lambda c: (1 - c,)), q_got)

    def along(r):
        def target(a, c):
            return (a + FAR[c][r]) % NZ, c

        return target

    came = [moved(chip, ("z", "co"), along(r)) for r in range(len(FAR[0]))]
    came.append(moved(pair, ("z",), lambda a: ((a + MIDDLE) % NZ,)))

    queries, bias, gate = pl.pallas_call(
        query_kernel,
        in_specs=[SMEM, SMEM, SMEM, VMEM, VMEM, HBM, ANY],
        out_specs=[VMEM] * 3,
        out_shape=[
            like((rows, width)),
            like((NY, keys), jnp.float32),
            like((2 * rows, share), jnp.float32),
        ],
        scratch_shapes=[pltpu.VMEM((8, share), jnp.float32), pltpu.SemaphoreType.DMA],
        compiler_params=room(6),
        name="q_heads",
    )(levels, frames, block_mask, q_mine, q_got, table, chip)
    asked = lax.all_gather(queries, "y")
    came = [after(c, asked) for c in came]
    beside = [moved(c, ("co",), lambda c: (1 - c,)) for c in came]

    partial = pl.pallas_call(
        attention_kernel,
        in_specs=[VMEM] * 11,
        out_specs=[VMEM] * NY,
        out_shape=[like((rows, width + STATS))] * NY,
        compiler_params=room(16),
        name="attention",
    )(asked, chip, *came, *beside, bias)
    parts = [partial[0]]
    for d in range(1, NY):
        parts.append(moved(partial[d], ("y",), lambda b, d=d: ((b - d) % NY,)))
    attended = pl.pallas_call(
        merge_kernel, out_shape=like((rows, width)), compiler_params=room(4), name="merge"
    )(*parts)

    same = moved(attended, ("xl", "co"), lambda s, c: (c, s))
    other = moved(attended, ("xl", "co"), lambda s, c: (1 - c, s))
    keep, give = pl.pallas_call(
        out_kernel,
        in_specs=[VMEM, VMEM, VMEM],
        out_specs=[VMEM, VMEM],
        out_shape=[like((2 * rows, share), jnp.float32), like((2 * rows, share))],
        compiler_params=room(10),
        name="out",
    )(same, other, out_weight)
    first, second = pl.pallas_call(
        pieces_kernel,
        in_specs=[VMEM] * 4,
        out_specs=[VMEM] * 2,
        out_shape=[like((rows, share))] * 2,
        compiler_params=room(6),
        name="pieces",
    )(keep, moved(give, ("co",), lambda c: (1 - c,)), gate, rest)

    def onward(k):
        def target(a, b, s, h):
            goal = next_owner(a, b)
            return None if goal is None else goal + (k ^ h, s)

        return target

    first = moved(first, ("z", "y", "xl", "xh"), onward(0))
    second = moved(second, ("z", "y", "xl", "xh"), onward(1))
    updated = (first.astype(jnp.float32) + second.astype(jnp.float32)).astype(jnp.bfloat16)
    return jnp.where(my_group() == 0, entering, updated)


def solution(mesh):
    fine = Mesh(mesh.devices.reshape(SIZES), AXES)
    tensor = ("xh", "co")
    placed = (
        P(("z", "y", "xl"), None),
        P("xl", tensor),
        P("xl", None, tensor),
        P(tensor, "xl"),
        P(tensor),
        P(tensor),
        P(),
        P(),
        P(),
        P(),
    )
    return jax.shard_map(
        per_device,
        mesh=fine,
        in_specs=placed,
        out_specs=P(("z", "y", "xl"), tensor),
        check_vma=False,
    )
```

```python
import functools
import math

import jax
import jax.numpy as jnp
import numpy as np
from jax import lax
from jax.experimental import pallas as pl
from jax.experimental.pallas import tpu as pltpu
from jax.sharding import Mesh, PartitionSpec as P

HDIM = 128
FT = 32
AXES = ("z", "y", "xl", "xh", "co")
SIZES = (8, 4, 2, 2, 2)
NZ, NY = 8, 4
HIDDEN = -(2.0**100)
STATS = 128
GAIN_ROWS = 16
FAR = ((1, 7, 3), (2, 6, 5))
MIDDLE = NZ // 2
SMEM = pl.BlockSpec(memory_space=pltpu.SMEM)
VMEM = pl.BlockSpec(memory_space=pltpu.VMEM)
ANY = pl.BlockSpec(memory_space=pl.ANY)
HBM = pl.BlockSpec(memory_space=pltpu.HBM)


def room(mib):
    return pltpu.CompilerParams(vmem_limit_bytes=mib * 1024 * 1024)


def my_group():
    return lax.axis_index("z") * NY + lax.axis_index("y")


def like(shape, dtype=jnp.bfloat16):
    return jax.ShapeDtypeStruct(shape, dtype)


def moved(value, axes, target):
    sizes = [SIZES[AXES.index(axis)] for axis in axes]
    pairs = []
    for place in np.ndindex(*sizes):
        goal = target(*place)
        if goal is not None:
            pairs.append((int(np.ravel_multi_index(place, sizes)), int(np.ravel_multi_index(goal, sizes))))
    return lax.ppermute(value, axes, pairs)


def next_owner(z, y):
    goal = z * NY + y + 1
    return None if goal == NZ * NY else divmod(goal, NY)


def after(value, *others):
    return pl.pallas_call(
        lambda *refs: None,
        in_specs=[ANY] * (1 + len(others)),
        out_specs=ANY,
        out_shape=like(value.shape, value.dtype),
        input_output_aliases={0: 0},
        compiler_params=room(1),
        name="after",
    )(value, *others)


def norm_kernel(levels_ref, stream_ref, table_ref, mine_ref, theirs_ref, change_ref, share_ref, levels, raw, held, sems):
    rows, model = raw.shape
    half, share = mine_ref.shape[1], share_ref.shape[1]
    whole = pltpu.make_async_copy(stream_ref, raw, sems.at[0])
    whole.start()
    first = pltpu.make_async_copy(levels_ref, levels, sems.at[2])
    first.start()
    first.wait()
    level = levels[my_group()]
    begin = pl.multiple_of((level // 8) * 8, 8)
    seq = lax.axis_index("xl")
    columns = pl.ds(pl.multiple_of(seq * half, 128), half)
    copy = pltpu.make_async_copy(table_ref.at[pl.ds(0, 2), pl.ds(begin, 8), columns], held, sems.at[1])
    copy.start()
    whole.wait()
    values = raw[...].astype(jnp.float32)
    center = jnp.mean(values, axis=-1, keepdims=True)
    centred = values - center
    spread = jnp.mean(centred * centred, axis=-1, keepdims=True)
    scale = lax.rsqrt(spread + 1e-06)
    lane = lax.broadcasted_iota(jnp.int32, (rows, STATS), 1)
    terms = jnp.zeros((rows, STATS), jnp.float32)
    for i, left in enumerate((center, scale)):
        for j in range(3):
            term = left.astype(jnp.bfloat16).astype(jnp.float32)
            terms = jnp.where(lane == 3 * i + j, term, terms)
            left = left - term
    quarter = (1 - seq) * half + lax.axis_index("co") * share
    theirs_ref[:, pl.ds(0, share)] = raw[:, pl.ds(pl.multiple_of(quarter, 128), share)]
    theirs_ref[:, pl.ds(share, STATS)] = terms.astype(jnp.bfloat16)
    copy.wait()
    row = pl.ds(lax.rem(level, 8), 1)
    change_ref[pl.ds(0, 1), :] = held[0, row, :]
    change_ref[pl.ds(1, 1), :] = 1.0 + held[1, row, :]
    own = raw[:, columns].astype(jnp.float32)
    mine_ref[...] = ((own - center) * scale * change_ref[1:2, :] + change_ref[0:1, :]).astype(jnp.bfloat16)
    place = (2 * seq + lax.axis_index("co")) * share
    share_ref[...] = raw[:, pl.ds(pl.multiple_of(place, 128), share)]


def set_up(levels, frames, block_mask, table_ref, bias_ref, gate_ref, held, sem):
    blocks, keys = bias_ref.shape
    rows, share = gate_ref.shape[0] // 2, gate_ref.shape[1]
    z, y, core = lax.axis_index("z"), lax.axis_index("y"), lax.axis_index("co")
    columns = pl.ds(pl.multiple_of((2 * lax.axis_index("xl") + core) * share, 128), share)
    level = levels[my_group()]
    aligned = pl.multiple_of((level // 8) * 8, 8)
    copy = pltpu.make_async_copy(table_ref.at[2, pl.ds(aligned, 8), columns], held, sem)
    copy.start()
    lane = lax.broadcasted_iota(jnp.int32, (1, keys), 1)
    for b in range(blocks):
        asker = z * NY + lax.rem(y + NY - b, NY)
        line = jnp.full((1, keys), HIDDEN, jnp.float32)
        for i in range(NZ):
            d = 0 if i == 0 else MIDDLE
            if 1 <= i <= 3:
                d = jnp.where(core == 0, FAR[0][i - 1], FAR[1][i - 1])
            elif 4 <= i <= 6:
                d = jnp.where(core == 0, FAR[1][i - 4], FAR[0][i - 4])
            block = lax.rem(z + NZ - d, NZ) * NY + y
            seen = (block == asker) | ((block < asker) & (block_mask[asker, block] == 1))
            count = jnp.where(seen, frames[block] * FT, 0)
            begin = i * (keys // NZ)
            line = jnp.where((lane >= begin) & (lane < begin + count), 0.0, line)
        bias_ref[pl.ds(b, 1), :] = line
    copy.wait()
    gate = held[pl.ds(lax.rem(level, 8), 1), :]
    row = lax.broadcasted_iota(jnp.int32, (rows, share), 0)
    for k in range(2):
        position = (lax.axis_index("xh") if k == 0 else 1 - lax.axis_index("xh")) * rows + row
        gate_ref[pl.ds(k * rows, rows), :] = jnp.where(position < frames[my_group()] * FT, gate, 0.0)


def terms_of(value, count):
    terms = []
    for _ in range(count):
        term = value.astype(jnp.bfloat16)
        terms.append(term)
        value = value - term.astype(jnp.float32)
    return terms


def project(tokens_ref, held, j, copies=None):
    depth = held.shape[1]
    steps = tokens_ref.shape[1] // depth
    total = None
    for i in range(steps):
        n = j * steps + i
        if copies is not None:
            copies[n].wait()
        part = tokens_ref[:, i * depth : (i + 1) * depth]
        term = jnp.dot(part, held[n], preferred_element_type=jnp.float32)
        total = term if total is None else total + term
    return total


def store_sums(out, *columns):
    rows, width = columns[0].shape
    for i, value in enumerate(columns):
        out[pl.ds(0, rows), pl.ds(i * width, width)] = value


def project_mine_kernel(tokens_ref, q_gain_in, k_gain_in, weight_ref, q_ref, kv_ref, held, q_gain_ref, k_gain_ref, sems):
    slots, depth, width = held.shape
    rows = tokens_ref.shape[0]
    small = [
        pltpu.make_async_copy(q_gain_in, q_gain_ref, sems.at[slots]),
        pltpu.make_async_copy(k_gain_in, k_gain_ref, sems.at[slots + 1]),
    ]
    for copy in small:
        copy.start()
    copies = []
    for n in range(slots):
        j, i = divmod(n, slots // 3)
        piece = weight_ref.at[j, pl.ds(i * depth, depth), :]
        copies.append(pltpu.make_async_copy(piece, held.at[n], sems.at[n]))
    for copy in copies:
        copy.start()
    for copy in small:
        copy.wait()
    gains = []
    for gain_ref in (k_gain_ref, q_gain_ref):
        gains += terms_of(gain_ref[...].reshape(1, width), 3)
    row = lax.broadcasted_iota(jnp.int32, (GAIN_ROWS, width), 0)
    for side in range(2):
        block = jnp.zeros((GAIN_ROWS, width), jnp.float32)
        for r in range(3):
            block = jnp.where(row == r, gains[2 * r + side].astype(jnp.float32), block)
        q_ref[pl.ds(rows, GAIN_ROWS), pl.ds(side * width, width)] = block.astype(jnp.bfloat16)
    store_sums(q_ref, *terms_of(project(tokens_ref, held, 0, copies), 2))
    key = project(tokens_ref, held, 1, copies)
    store_sums(kv_ref, *terms_of(key, 2), project(tokens_ref, held, 2, copies).astype(jnp.bfloat16))


def project_kv_kernel(got_ref, sib_ref, change_ref, share_ref, held, kv_ref, tokens_ref, rest_ref):
    share = share_ref.shape[1]
    core = lax.axis_index("co")
    terms = got_ref[:, pl.ds(share, STATS)].astype(jnp.float32)
    center = terms[:, 0:1] + terms[:, 1:2] + terms[:, 2:3]
    scale = terms[:, 3:4] + terms[:, 4:5] + terms[:, 5:6]
    for ref, at in ((got_ref, core), (sib_ref, 1 - core)):
        columns = pl.ds(pl.multiple_of(at * share, 128), share)
        centred = ref[:, pl.ds(0, share)].astype(jnp.float32) - center
        normed = centred * scale * change_ref[pl.ds(1, 1), columns] + change_ref[pl.ds(0, 1), columns]
        tokens_ref[:, columns] = normed.astype(jnp.bfloat16)
    other = got_ref[:, pl.ds(0, share)]
    rest_ref[...] = jnp.where(lax.axis_index("xh") == lax.axis_index("xl"), share_ref[...], other)
    key = project(tokens_ref, held, 1)
    store_sums(kv_ref, *terms_of(key, 2), project(tokens_ref, held, 2).astype(jnp.bfloat16))


def project_q_kernel(tokens_ref, held, q_ref):
    store_sums(q_ref, *terms_of(project(tokens_ref, held, 0), 2))


def head_norm(values, gain):
    square = jnp.mean(values * values, axis=-1, keepdims=True)
    return (values * lax.rsqrt(square + 1e-06) * gain).astype(jnp.bfloat16)


def wide(ref, *places):
    return sum(ref[place].astype(jnp.float32) for place in places)


def gain_of(which, q_ref, rows, h):
    width = q_ref.shape[1] // 2
    gain = 0.0
    for p in range(3 * which, 3 * which + 3):
        columns = pl.ds((p % 2) * width + h * HDIM, HDIM)
        block = q_ref[pl.ds(rows, GAIN_ROWS), columns].astype(jnp.float32)
        gain = gain + block[p // 2 : p // 2 + 1]
    return gain


def sum_of(a_ref, b_ref, rows, blocks, width, h):
    at = [(pl.ds(0, rows), pl.ds(i * width + h * HDIM, HDIM)) for i in blocks]
    return wide(a_ref, *at) + wide(b_ref, *at)


def kv_kernel(a_ref, b_ref, q_ref, waits_ref, out_ref):
    rows, width = out_ref.shape[0], out_ref.shape[1] // 2
    for h in range(width // HDIM):
        key = sum_of(a_ref, b_ref, rows, (0, 1), width, h)
        out_ref[:, pl.ds(h * HDIM, HDIM)] = head_norm(key, gain_of(0, q_ref, rows, h))
        value = sum_of(a_ref, b_ref, rows, (2,), width, h)
        out_ref[:, pl.ds(width + h * HDIM, HDIM)] = value.astype(jnp.bfloat16)


def query_kernel(levels, frames, block_mask, a_ref, b_ref, table_ref, waits_ref, out_ref, *rest):
    rows, width = out_ref.shape
    for h in range(width // HDIM):
        query = sum_of(a_ref, b_ref, rows, (0, 1), width, h)
        out_ref[:, pl.ds(h * HDIM, HDIM)] = head_norm(query, gain_of(1, a_ref, rows, h))
    set_up(levels, frames, block_mask, table_ref, *rest)


def chip_kernel(own_ref, sib_ref, waits_ref, out_ref):
    rows = own_ref.shape[0]
    core = lax.axis_index("co")
    out_ref[pl.ds(pl.multiple_of(core * rows, rows), rows), :] = own_ref[...]
    out_ref[pl.ds(pl.multiple_of((1 - core) * rows, rows), rows), :] = sib_ref[...]


def attention_kernel(*refs):
    asked_ref, own, came, beside, bias_ref, outs = refs[0], refs[1], refs[2:6], refs[6:10], refs[10], refs[-NY:]
    rows, width = asked_ref.shape[1:]
    keys_in = [own, *came[:3], *beside[:3]]
    y = lax.axis_index("y")
    asked = [asked_ref.at[lax.rem(y + NY - b, NY)] for b in range(NY)]
    first = lax.axis_index("co") == 0

    def rows_of(at):
        own_half, other_half = came[3][:, at], beside[3][:, at]
        last = [jnp.where(first, own_half, other_half), jnp.where(first, other_half, own_half)]
        return jnp.concatenate([r[:, at] for r in keys_in] + last, axis=0)

    keys = bias_ref.shape[1]
    blocks = len(asked)
    bias = jnp.concatenate(
        [jnp.broadcast_to(bias_ref[b : b + 1, :], (rows, keys)) for b in range(blocks)], axis=0
    )
    stats = []
    for h in range(width // HDIM):
        at = pl.ds(h * HDIM, HDIM)
        past = pl.ds(width + h * HDIM, HDIM)
        q = jnp.concatenate([r[:, at] for r in asked], axis=0)
        k = rows_of(at)
        v = rows_of(past)
        scores = lax.dot_general(q, k, (((1,), (1,)), ((), ())), preferred_element_type=jnp.float32)
        scores = scores * (1.0 / math.sqrt(HDIM)) + bias
        top = jnp.max(scores, axis=1, keepdims=True).astype(jnp.bfloat16).astype(jnp.float32)
        weights = jnp.exp(scores - top)
        total = jnp.sum(weights, axis=1, keepdims=True)
        mixed = jnp.dot(weights.astype(jnp.bfloat16), v, preferred_element_type=jnp.float32)
        mixed = mixed.astype(jnp.bfloat16)
        for b, out in enumerate(outs):
            out[:, at] = mixed[b * rows : (b + 1) * rows]
        high = total.astype(jnp.bfloat16).astype(jnp.float32)
        stats += [top, high, total - high]
    lane = lax.broadcasted_iota(jnp.int32, (blocks * rows, STATS), 1)
    packed = jnp.zeros((blocks * rows, STATS), jnp.float32)
    for i, s in enumerate(stats):
        packed = jnp.where(lane == i, s, packed)
    packed = packed.astype(jnp.bfloat16)
    for b, out in enumerate(outs):
        out[:, pl.ds(width, STATS)] = packed[b * rows : (b + 1) * rows]


def merge_kernel(a_ref, b_ref, c_ref, d_ref, out_ref):
    width = out_ref.shape[1]
    parts = (a_ref, b_ref, c_ref, d_ref)
    stats = [p[:, pl.ds(width, STATS)].astype(jnp.float32) for p in parts]
    for h in range(width // HDIM):
        at = pl.ds(h * HDIM, HDIM)
        tops = [s[:, 3 * h : 3 * h + 1] for s in stats]
        sums = [s[:, 3 * h + 1 : 3 * h + 2] + s[:, 3 * h + 2 : 3 * h + 3] for s in stats]
        top = functools.reduce(jnp.maximum, tops)
        scales = [jnp.exp(t - top) for t in tops]
        total = sum(s * w for s, w in zip(sums, scales))
        mixed = sum(p[:, at].astype(jnp.float32) * w for p, w in zip(parts, scales))
        out_ref[:, at] = (mixed / total).astype(jnp.bfloat16)


def out_kernel(same_ref, other_ref, weight_ref, keep_ref, first_ref, second_ref):
    rows, share = same_ref.shape[0], keep_ref.shape[1]
    swap = lax.axis_index("xl") != lax.axis_index("xh")
    same, other = same_ref[...], other_ref[...]
    tokens = jnp.concatenate([jnp.where(swap, other, same), jnp.where(swap, same, other)], axis=0)
    core = lax.axis_index("co")
    near = weight_ref[:, pl.ds(pl.multiple_of(core * share, 128), share)]
    give = weight_ref[:, pl.ds(pl.multiple_of((1 - core) * share, 128), share)]
    given = jnp.dot(tokens, give, preferred_element_type=jnp.float32).astype(jnp.bfloat16)
    first_ref[...] = given[:rows]
    second_ref[...] = given[rows:]
    keep_ref[...] = jnp.dot(tokens, near, preferred_element_type=jnp.float32)


def first_kernel(keep_ref, got_ref, gate_ref, rest_ref, out_ref):
    rows = out_ref.shape[0]
    summed = keep_ref[pl.ds(0, rows), :] + got_ref[...].astype(jnp.float32)
    change = gate_ref[pl.ds(0, rows), :] * summed
    out_ref[...] = (rest_ref[...].astype(jnp.float32) + change).astype(jnp.bfloat16)


def second_kernel(keep_ref, got_ref, gate_ref, out_ref):
    rows = out_ref.shape[0]
    summed = keep_ref[pl.ds(rows, rows), :] + got_ref[...].astype(jnp.float32)
    out_ref[...] = (gate_ref[pl.ds(rows, rows), :] * summed).astype(jnp.bfloat16)


def per_device(
    stream, entering, qkv_weight, out_weight, q_gain, k_gain, mod_table, levels, frames, block_mask
):
    rows, model = stream.shape
    width = q_gain.shape[0]
    half, share = model // 2, model // 4
    keys = 2 * NZ * rows
    table = pltpu.with_memory_space_constraint(jnp.transpose(mod_table, (1, 0, 2)), pltpu.HBM)
    weight = pltpu.with_memory_space_constraint(jnp.transpose(qkv_weight, (1, 0, 2)), pltpu.HBM)

    mine, theirs, change, part = pl.pallas_call(
        norm_kernel,
        in_specs=[HBM, HBM, HBM],
        out_specs=[VMEM] * 4,
        out_shape=[
            like((rows, half)),
            like((rows, share + STATS)),
            like((2, half), jnp.float32),
            like((rows, share)),
        ],
        scratch_shapes=[
            pltpu.SMEM(levels.shape, jnp.int32),
            pltpu.VMEM((rows, model), jnp.bfloat16),
            pltpu.VMEM((2, 8, half), jnp.float32),
            pltpu.SemaphoreType.DMA((3,)),
        ],
        compiler_params=room(8),
        name="norm",
    )(
        pltpu.with_memory_space_constraint(levels, pltpu.HBM),
        pltpu.with_memory_space_constraint(stream, pltpu.HBM),
        table,
    )
    theirs = moved(theirs, ("xl",), lambda s: (1 - s,))

    slots = 12
    q_mine, kv_mine, kept = pl.pallas_call(
        project_mine_kernel,
        in_specs=[VMEM, HBM, HBM, HBM],
        out_specs=[VMEM] * 3,
        out_shape=[
            like((rows + GAIN_ROWS, 2 * width)),
            like((rows, 3 * width)),
            like((slots, 3 * half // slots, width)),
        ],
        scratch_shapes=[
            pltpu.VMEM((width,), jnp.float32),
            pltpu.VMEM((width,), jnp.float32),
            pltpu.SemaphoreType.DMA((slots + 2,)),
        ],
        compiler_params=room(16),
        name="project_mine",
    )(
        mine,
        pltpu.with_memory_space_constraint(q_gain, pltpu.HBM),
        pltpu.with_memory_space_constraint(k_gain, pltpu.HBM),
        weight,
    )
    theirs = after(theirs, kept)
    kv_mine = moved(kv_mine, ("xl", "co"), lambda s, c: (c, s))
    q_mine = moved(q_mine, ("xl", "co"), lambda s, c: (c, s))
    kv_got, got, rest = pl.pallas_call(
        project_kv_kernel,
        in_specs=[VMEM] * 5,
        out_specs=[VMEM] * 3,
        out_shape=[like((rows, 3 * width)), like((rows, half)), like((rows, share))],
        compiler_params=room(14),
        name="project_kv",
    )(theirs, moved(theirs, ("co",), lambda c: (1 - c,)), change, part, kept)
    kv_got = moved(kv_got, ("xl", "co"), lambda s, c: (c, 1 - s))
    q_got = pl.pallas_call(
        project_q_kernel,
        in_specs=[VMEM] * 2,
        out_specs=VMEM,
        out_shape=like((rows, 2 * width)),
        compiler_params=room(14),
        name="project_q",
    )(got, kept)
    pair = pl.pallas_call(
        kv_kernel,
        in_specs=[VMEM, VMEM, VMEM, ANY],
        out_specs=VMEM,
        out_shape=like((rows, 2 * width)),
        compiler_params=room(4),
        name="kv_heads",
    )(kv_mine, kv_got, q_mine, q_got)
    q_got = moved(q_got, ("xl", "co"), lambda s, c: (c, 1 - s))

    chip = pl.pallas_call(
        chip_kernel,
        in_specs=[VMEM, VMEM, ANY],
        out_specs=VMEM,
        out_shape=like((2 * rows, 2 * width)),
        compiler_params=room(4),
        name="chip",
    )(pair, moved(pair, ("co",), lambda c: (1 - c,)), q_got)

    def along(r):
        def target(a, c):
            return (a + FAR[c][r]) % NZ, c

        return target

    came = [moved(chip, ("z", "co"), along(r)) for r in range(len(FAR[0]))]
    came.append(moved(pair, ("z",), lambda a: ((a + MIDDLE) % NZ,)))

    queries, bias, gate = pl.pallas_call(
        query_kernel,
        in_specs=[SMEM, SMEM, SMEM, VMEM, VMEM, HBM, ANY],
        out_specs=[VMEM] * 3,
        out_shape=[
            like((rows, width)),
            like((NY, keys), jnp.float32),
            like((2 * rows, share), jnp.float32),
        ],
        scratch_shapes=[pltpu.VMEM((8, share), jnp.float32), pltpu.SemaphoreType.DMA],
        compiler_params=room(6),
        name="q_heads",
    )(levels, frames, block_mask, q_mine, q_got, table, chip)
    asked = lax.all_gather(queries, "y")
    came = [after(c, asked) for c in came]
    beside = [moved(c, ("co",), lambda c: (1 - c,)) for c in came]

    partial = pl.pallas_call(
        attention_kernel,
        in_specs=[VMEM] * 11,
        out_specs=[VMEM] * NY,
        out_shape=[like((rows, width + STATS))] * NY,
        compiler_params=room(16),
        name="attention",
    )(asked, chip, *came, *beside, bias)
    parts = [partial[0]]
    for d in range(1, NY):
        parts.append(moved(partial[d], ("y",), lambda b, d=d: ((b - d) % NY,)))
    attended = pl.pallas_call(
        merge_kernel, out_shape=like((rows, width)), compiler_params=room(4), name="merge"
    )(*parts)

    same = moved(attended, ("xl", "co"), lambda s, c: (c, s))
    other = moved(attended, ("xl", "co"), lambda s, c: (1 - c, s))
    keep, give_first, give_second = pl.pallas_call(
        out_kernel,
        in_specs=[VMEM, VMEM, VMEM],
        out_specs=[VMEM] * 3,
        out_shape=[like((2 * rows, share), jnp.float32), like((rows, share)), like((rows, share))],
        compiler_params=room(10),
        name="out",
    )(same, other, out_weight)
    def piece(kernel, given, *others):
        return pl.pallas_call(
            kernel,
            out_shape=like((rows, share)),
            compiler_params=room(6),
            name="piece",
        )(keep, moved(given, ("co",), lambda c: (1 - c,)), gate, *others)

    first, second = piece(first_kernel, give_first, rest), piece(second_kernel, give_second)

    def onward(k):
        def target(a, b, s, h):
            goal = next_owner(a, b)
            return None if goal is None else goal + (k ^ h, s)

        return target

    first = moved(first, ("z", "y", "xl", "xh"), onward(0))
    second = moved(second, ("z", "y", "xl", "xh"), onward(1))
    updated = (first.astype(jnp.float32) + second.astype(jnp.float32)).astype(jnp.bfloat16)
    return jnp.where(my_group() == 0, entering, updated)


def solution(mesh):
    fine = Mesh(mesh.devices.reshape(SIZES), AXES)
    tensor = ("xh", "co")
    placed = (
        P(("z", "y", "xl"), None),
        P("xl", tensor),
        P("xl", None, tensor),
        P(tensor, "xl"),
        P(tensor),
        P(tensor),
        P(),
        P(),
        P(),
        P(),
    )
    return jax.shard_map(
        per_device,
        mesh=fine,
        in_specs=placed,
        out_specs=P(("z", "y", "xl"), tensor),
        check_vma=False,
    )
```
